256 devices in a mesh: dp: 128 (over y, x, z), rep: 2 (over core).
Axes of the slice: x: 4, y: 4, z: 8, core: 2. Of those that a mesh axis runs over, the one named last changes fastest.
Arguments:
- embeddings: bfloat16 [32768, 1024], P(('dp', 'rep')), may hold values from -15 to 15
- parents: int32 [32768], P(('dp', 'rep')), may hold values from 0 to 63, as said below
- block_lists: int32 [64, 16], replicated, may hold values from 0 to 1023, as said below
- centroids: bfloat16 [262144, 1024], P('dp'), may hold values from -6.5 to 6.5
Outputs:
- new_centroids: float32 [262144, 1024], P('dp', 'rep')
- spread: float32 [32768], P(('dp', 'rep'))
The draws below stay inside these ranges and needn't reach their ends.
Inputs may be any that keep to these rules, and one draw needn't show every extreme that they name: `parents`: among the 128 embeddings of one device at most 4 share a parent, and on every device some parent has exactly 4. `block_lists`: each of the 1024 blocks stands in exactly one parent's list.
All inputs are finite; a program needn't handle non-finite values.
Results may differ from the reference program's by a relative error of at most 0.0017.
Values may be sent and summed in bfloat16 or wider, within the bound.
A program may use at most 128 MiB of HBM per device.

```python
import math
import jax
import jax.numpy as jnp
from jax import lax

D = 1024
BS = 256
LIST = 16
E_DEV = 128
NB = 1024
PARENTS = 64
CAP = 4
CENT = 262144
EMB = 32768


def block_order(key):
    return jax.random.permutation(jax.random.fold_in(key, 7), NB).astype(jnp.int32).reshape(PARENTS, LIST)


def parent_draw(key):
    stream = jax.random.fold_in(key, 11)
    labels = jnp.arange(PARENTS * CAP, dtype=jnp.int32) // CAP

    def device_rows(index):
        device_key = jax.random.fold_in(stream, index)
        leader_key, order_key, shuffle_key = jax.random.split(device_key, 3)
        leader = jax.random.randint(leader_key, (), 0, PARENTS).astype(jnp.int32)
        shuffled = labels[jax.random.permutation(order_key, PARENTS * CAP)]
        ranking = jnp.argsort(jnp.where(shuffled == leader, 0, 1).astype(jnp.int32), stable=True)
        chosen = shuffled[ranking][:E_DEV]
        return jax.random.permutation(shuffle_key, chosen)
    return jax.vmap(device_rows)(jnp.arange(EMB // E_DEV)).reshape(EMB).astype(jnp.int32)


def centroid_rows(key, indices):
    stream = jax.random.fold_in(key, 5)

    def one_row(index):
        return jnp.clip(jax.random.normal(jax.random.fold_in(stream, index), (D,), jnp.float32), -6.0, 6.0)
    return jax.vmap(one_row)(indices)


def draw_parents(key, part):
    chosen = parent_draw(key)
    return chosen


def draw_block_lists(key, part):
    ordered = block_order(key)
    return ordered


def draw_centroids(key, part):
    vectors = centroid_rows(key, jnp.arange(CENT))
    return vectors.astype(jnp.bfloat16)


def draw_embeddings(key, part):
    own_key = jax.random.fold_in(key, 31)
    vectors = jnp.clip(jax.random.normal(own_key, (EMB, D), jnp.float32), -6.0, 6.0)
    return vectors.astype(jnp.bfloat16)


def setup_inputs(seed: int = 0) -> dict:
    streams_of = jax.random.split(jax.random.key(seed), 5)
    embeddings = draw_embeddings(jax.random.fold_in(streams_of[4], 71), 0)
    parents = draw_parents(jax.random.fold_in(streams_of[4], 71), 0)
    block_lists = draw_block_lists(jax.random.fold_in(streams_of[4], 71), 0)
    centroids = draw_centroids(jax.random.fold_in(streams_of[4], 71), 0)
    return {"embeddings": embeddings, "parents": parents, "block_lists": block_lists, "centroids": centroids}


BETA = 3.0
LAMBDA = 0.25

def reference(embeddings, parents, block_lists, centroids):
    ordering = jnp.argsort(parents, stable=True).astype(jnp.int32)
    counts = lax.optimization_barrier(jnp.sum((parents[:, None] == jnp.arange(PARENTS, dtype=jnp.int32)[None, :]).astype(jnp.int32), axis=0))
    starts = jnp.cumsum(counts) - counts
    widest = CAP * (EMB // E_DEV)
    grouped = centroids.reshape(NB, BS, D)
    scale = BETA / math.sqrt(D)

    def per_parent(parent):
        offsets = jnp.arange(widest, dtype=jnp.int32)
        valid = offsets < counts[parent]
        members = ordering[jnp.minimum(starts[parent] + offsets, EMB - 1)]
        vectors = embeddings[members]
        candidates = grouped[block_lists[parent]].reshape(LIST * BS, D)
        scores = jnp.dot(vectors, candidates.T, preferred_element_type=jnp.float32) * scale
        highest = lax.optimization_barrier(jnp.max(scores, axis=1, keepdims=True))
        summed = lax.optimization_barrier(jnp.sum(jnp.exp(scores - highest), axis=1, keepdims=True))
        lognorm = highest + jnp.log(summed)
        weights = jnp.exp(scores - lognorm) * valid[:, None].astype(jnp.float32)
        masses = lax.optimization_barrier(jnp.sum(weights, axis=0))
        sum_rows = jnp.dot(weights.astype(jnp.bfloat16).T, vectors, preferred_element_type=jnp.float32)
        updated = (sum_rows + LAMBDA * candidates.astype(jnp.float32)) / (masses[:, None] + LAMBDA)
        targets = jnp.where(valid, members, EMB).astype(jnp.int32)
        return (updated, jnp.log(summed[:, 0]), targets)
    updated, spreads, targets = lax.map(per_parent, jnp.arange(PARENTS, dtype=jnp.int32))
    spread = jnp.zeros((EMB,), jnp.float32).at[targets.reshape(-1)].set(spreads.reshape(-1), mode='drop')
    location = jnp.argsort(block_lists.reshape(-1)).astype(jnp.int32)
    new_centroids = updated.reshape(NB, BS, D)[location].reshape(CENT, D)
    return (new_centroids, spread)
```

```python
import math

import jax
import jax.numpy as jnp
from jax import lax
from jax.experimental import pallas as pl
from jax.experimental.pallas import tpu as pltpu
from jax.sharding import PartitionSpec as P

BETA = 3.0
LAMBDA = 0.25
EMPTY_NORM = 1e30
NONE_MAX = -1e30
MESH = pl.DeviceIdType.MESH

NY, NX, NZ, NC = 4, 4, 8, 2
ROWS = 128
D = 1024
HALF = 512
BS = 256
OWN = 4
CAP = 4
F32 = jnp.float32
BF16 = jnp.bfloat16


def kernel(
    emb, par, bl, cent, out, spread,
    raw, slz, slp, pk, inc, ce, e_sc, ms, ss, stt, rs, tz, lt, lr, wb, fr, keys, pbq,
    s_zs, s_zr, s_as, s_ar, s_slzs, s_slzr, s_slps, s_slpr, s_ps, s_pr, s_loc, s_ce,
    s_sts, s_str, s_tzs, s_tzr, s_ls, s_lr, s_fs, s_fr, s_fl,
):
    dp = lax.axis_index("dp")
    c = lax.axis_index("rep")
    y = dp // 32
    x = (dp // 8) % 4
    z = dp % 8

    def chip(yy, xx, zz):
        return (yy * 4 + xx) * 8 + zz

    def zdev(dz):
        return (chip(y, x, (z + dz) % 8), c)

    def adev(p, k, dc=0):
        return (chip((y + k) % 4, x, z) if p == 0 else chip(y, (x + k) % 4, z), c)

    def bdev(p, k, dc):
        cc = (c + dc) % 2
        return (chip(y, (x + k) % 4, z) if p == 0 else chip((y + k) % 4, x, z), cc)

    def plane(t):
        yy, xx, cc = (y + t // 8) % 4, (x + (t // 2) % 4) % 4, (c + t % 2) % 2
        return (chip(yy, xx, z), cc), (yy * 4 + xx) * 2 + cc

    my_u = (y * 4 + x) * 2 + c

    ce_copy = pltpu.make_async_copy(cent.at[pl.ds(c * 1024, 1024)], ce, s_ce)
    ce_copy.start()

    barrier = pltpu.get_barrier_semaphore()

    def greet(t, carry):
        dev, _ = plane(t)
        pl.semaphore_signal(barrier, 1, device_id=dev, device_id_type=MESH)
        return carry

    lax.fori_loop(1, 32, greet, 0)
    for dz in range(1, 8):
        pl.semaphore_signal(barrier, 1, device_id=zdev(dz), device_id_type=MESH)
    for p in range(2):
        raw[p, 0, 1] = emb[:, p * HALF:(p + 1) * HALF]
    pl.semaphore_wait(barrier, 38)

    def zsend(p, pos, step):
        to = (pos + 1) % 8 if step < 0 else (pos - 1) % 8
        pltpu.make_async_remote_copy(
            src_ref=raw.at[p, 0, pos], dst_ref=raw.at[p, 0, to],
            send_sem=s_zs.at[p], recv_sem=s_zr.at[p, to],
            device_id=zdev(step), device_id_type=MESH,
        ).start()

    def asend(p, pos):
        for k in (1, 3, 2):
            to = (-k) % 4
            pltpu.make_async_remote_copy(
                src_ref=raw.at[p, 0, pos], dst_ref=raw.at[p, to, pos],
                send_sem=s_as.at[p], recv_sem=s_ar.at[p, to, pos // 4],
                device_id=adev(p, k), device_id_type=MESH,
            ).start()

    def zwait(p, pos):
        pltpu.make_async_copy(raw.at[p, 0, pos], raw.at[p, 0, pos], s_zr.at[p, pos]).wait()

    for p in range(2):
        zsend(p, 1, -1)
        zsend(p, 1, 1)
    for p in range(2):
        asend(p, 1)

    par_row = par[0:1, :]
    sub = lax.broadcasted_iota(jnp.int32, (ROWS, ROWS), 0)
    lane = lax.broadcasted_iota(jnp.int32, (ROWS, ROWS), 1)
    par_wide = jnp.broadcast_to(par_row, (ROWS, ROWS))
    par_col = jnp.sum(jnp.where(sub == lane, par_wide, 0.0), axis=1, keepdims=True)
    earlier = jnp.where((par_col == par_wide) & (sub < lane), 1.0, 0.0)
    slot_row = par_row * CAP + jnp.sum(earlier, axis=0, keepdims=True)
    slot_col = jnp.sum(
        jnp.where(sub == lane, jnp.broadcast_to(slot_row, (ROWS, ROWS)), 0.0), axis=1, keepdims=True
    )
    slz[1, 0:8, :] = jnp.broadcast_to(slot_row, (8, 128))
    code = ((lane // 32) * CAP + lane % CAP).astype(F32)
    for p4 in range(16):
        hit = jnp.where(slot_col == code + float(16 * p4), 1.0, 0.0)
        slz[1, 8 + p4:9 + p4, :] = jnp.sum(hit, axis=0, keepdims=True)
    for dz in range(1, 8):
        to = (1 - dz) % 8
        pltpu.make_async_remote_copy(
            src_ref=slz.at[1], dst_ref=slz.at[to], send_sem=s_slzs, recv_sem=s_slzr,
            device_id=zdev(dz), device_id_type=MESH,
        ).start()

    def lookup(ids):
        n = ids.shape[0]
        acc = jnp.zeros((n, 128), F32)
        for ch in range(8):
            place = lax.broadcasted_iota(jnp.int32, (1, 128), 1) + ch * 128
            acc += jnp.where(ids == bl[ch:ch + 1, :], (place // 16).astype(F32), 0.0)
        return jnp.sum(acc, axis=1, keepdims=True)

    row = lax.broadcasted_iota(jnp.int32, (512, 1), 0)
    zz = (row // 4) % 4
    core = (row // 64) % 2
    core = jnp.where(core == 0, c, 1 - c)
    for p in range(2):
        far = row // 128
        where_to = chip(y, (x + far) % 4, z) if p == 0 else chip((y + far) % 4, x, z)
        ids = where_to * 8 + core * 4 + (row // 16) % 4
        keys[p] = jnp.broadcast_to(
            lookup(ids) * CAP + (row % 4).astype(F32) + (zz * 256).astype(F32), (512, 128)
        )
    r128 = lax.broadcasted_iota(jnp.int32, (128, 1), 0)
    peer = r128 % 32
    peer_chip = (peer // 2) * 8 + z
    wide = jnp.zeros((128, 128), F32)
    for q in range(4):
        ids = peer_chip * 8 + (peer % 2) * 4 + (q + 4 - r128 // 32) % 4
        wide = jnp.where(lane // 32 == q, lookup(ids) - float(q), wide)
    pbq[...] = wide

    for p in range(2):
        zwait(p, 2)
        zsend(p, 2, -1)
        zwait(p, 0)
        zsend(p, 0, 1)
    for p in range(2):
        asend(p, 2)
        asend(p, 0)
    pltpu.make_async_copy(slz.at[0:7], slz.at[0:7], s_slzr).wait()
    for p in range(2):
        for k in (1, 3, 2):
            to = (-k) % 4
            pltpu.make_async_remote_copy(
                src_ref=slz.at[:, 0:8, :], dst_ref=slp.at[p, to - 1],
                send_sem=s_slps.at[p], recv_sem=s_slpr.at[p],
                device_id=adev(p, k), device_id_type=MESH,
            ).start()
    for p in range(2):
        zwait(p, 3)
        zsend(p, 3, -1)
        zwait(p, 7)
        zsend(p, 7, 1)
    for p in range(2):
        asend(p, 3)
        asend(p, 7)
    for p in range(2):
        zwait(p, 4)
        zwait(p, 6)
        zsend(p, 4, -1) if p == 0 else zsend(p, 6, 1)
    for p in range(2):
        asend(p, 4)
        asend(p, 6)
    for p in range(2):
        zwait(p, 5)
        asend(p, 5)

    for p in range(2):
        pltpu.make_async_copy(slp.at[p], slp.at[p], s_slpr.at[p]).wait()

    def pack(p, g, k):
        n = g * 4 + k
        if k > 0:
            pltpu.make_async_copy(
                raw.at[p, k, pl.ds(4 * g, 4)], raw.at[p, k, pl.ds(4 * g, 4)], s_ar.at[p, k, g]
            ).wait()
        key = keys[p][:, 0:1]
        picks = []
        for w in range(4):
            s_row = slz[4 * g + w, 0:1, :] if k == 0 else slp[p, k - 1, 4 * g + w, 0:1, :]
            picks.append(jnp.where(key == s_row + float(256 * w), 1.0, 0.0).astype(BF16))
        pick = jnp.concatenate(picks, axis=1)
        rows = raw[p, k, 4 * g:4 * g + 4].reshape(512, HALF)
        packed = jnp.dot(pick, rows, preferred_element_type=F32).astype(BF16)
        pk[p, n] = packed.reshape(8, OWN, 16, HALF)
        u = (((y + k) % 4) * 4 + x) * 2 + c if p == 0 else (y * 4 + (x + k) % 4) * 2 + c
        off = pl.multiple_of((u % 8) * 128 + (u // 8) * 32 + g * 16, 16)
        dst = inc.at[:, pl.ds(off, 16), p * HALF:(p + 1) * HALF]
        for far in (1, 3, 2, 0):
            for dc in range(2):
                i = far * 2 + dc
                if i == 0:
                    pltpu.make_async_copy(pk.at[p, n, 0], dst, s_loc.at[p]).start()
                else:
                    pltpu.make_async_remote_copy(
                        src_ref=pk.at[p, n, i], dst_ref=dst,
                        send_sem=s_ps.at[p], recv_sem=s_pr.at[p],
                        device_id=bdev(p, far, dc), device_id_type=MESH,
                    ).start()

    for g in range(2):
        for k in (0, 1, 3, 2):
            for p in range(2):
                pack(p, g, k)

    ce_copy.wait()
    for p in range(2):
        got = inc.at[:, 0:896, p * HALF:(p + 1) * HALF]
        pltpu.make_async_copy(got, got, s_pr.at[p]).wait()
        pltpu.make_async_copy(pk.at[p, :, 0], pk.at[p, :, 0], s_loc.at[p]).wait()

    scale = BETA / math.sqrt(D)

    def score(j, carry):
        for n in range(4):
            s = lax.dot_general(
                ce[pl.ds(pl.multiple_of(j * BS, BS), BS), :], inc[j, n * 256:(n + 1) * 256, :],
                (((1,), (1,)), ((), ())), preferred_element_type=F32,
            ) * scale
            top = jnp.max(s, axis=0, keepdims=True)
            e = jnp.exp(s - top)
            e_sc[j, n] = e
            total = jnp.sum(e, axis=0, keepdims=True)
            for h in range(2):
                ms[j, 2 * n + h:2 * n + h + 1, :] = top[:, h * 128:(h + 1) * 128]
                ss[j, 2 * n + h:2 * n + h + 1, :] = total[:, h * 128:(h + 1) * 128]
        return carry

    lax.fori_loop(0, OWN, score, 0)

    group = lax.broadcasted_iota(jnp.int32, (8, 128), 1) // 32
    for q in range(4):
        tops, totals = ms[q], ss[q]
        for j in range(4):
            if j != q:
                turn = (32 * (j - q)) % 128
                tops = jnp.where(group == j, pltpu.roll(ms[j], turn, 1), tops)
                totals = jnp.where(group == j, pltpu.roll(ss[j], turn, 1), totals)
        for v in range(8):
            stt[8 * q + v, 0:1, :] = tops[v:v + 1, :]
            stt[8 * q + v, 1:2, :] = totals[v:v + 1, :]
    rs[my_u] = stt[my_u]

    def send_stats(t, carry):
        dev, u = plane(t)
        pltpu.make_async_remote_copy(
            src_ref=stt.at[u], dst_ref=rs.at[my_u], send_sem=s_sts, recv_sem=s_str,
            device_id=dev, device_id_type=MESH,
        ).start()
        return carry

    lax.fori_loop(1, 32, send_stats, 0)
    pltpu.make_async_copy(rs.at[0:31], rs.at[0:31], s_str).wait()

    m_in = jnp.concatenate([rs[d, 0:1, :] for d in range(32)], axis=0)
    s_in = jnp.concatenate([rs[d, 1:2, :] for d in range(32)], axis=0)
    m_all = jnp.concatenate([m_in] + [pltpu.roll(m_in, 32 * k, 1) for k in (1, 2, 3)], axis=0)
    s_all = jnp.concatenate([s_in] + [pltpu.roll(s_in, 32 * k, 1) for k in (1, 2, 3)], axis=0)
    owner = pbq[...]
    m_back = jnp.zeros((128, 128), F32)
    for p4 in range(16):
        mine = owner == float(4 * p4)
        top = jnp.max(jnp.where(mine, m_all, NONE_MAX), axis=0, keepdims=True)
        tz[0, 0, p4:p4 + 1, :] = top
        m_back = jnp.where(mine, top, m_back)
    z_all = s_all * jnp.exp(m_all - m_back)
    for p4 in range(16):
        mine = owner == float(4 * p4)
        tz[0, 1, p4:p4 + 1, :] = jnp.sum(jnp.where(mine, z_all, 0.0), axis=0, keepdims=True)

    for dz in range(1, 8):
        pltpu.make_async_remote_copy(
            src_ref=tz.at[0], dst_ref=tz.at[8 - dz], send_sem=s_tzs, recv_sem=s_tzr,
            device_id=zdev(dz), device_id_type=MESH,
        ).start()
    place = lax.broadcasted_iota(jnp.int32, (16, 128), 1) % 32
    filled = jnp.zeros((16, 128), F32)
    for pos in range(8):
        filled = jnp.where(place // 4 == pos, slz[pos, 8:24, :], filled)
    pltpu.make_async_copy(tz.at[1:8], tz.at[1:8], s_tzr).wait()

    def aligned(dz, what):
        t = tz[dz, what]
        if dz == 0:
            return t
        turn = 4 * dz
        return jnp.where(place >= turn, pltpu.roll(t, turn, 1), pltpu.roll(t, 96 + turn, 1))

    tops = [aligned(dz, 0) for dz in range(8)]
    highest = tops[0]
    for t in tops[1:]:
        highest = jnp.maximum(highest, t)
    summed = jnp.zeros((16, 128), F32)
    for dz in range(8):
        summed += aligned(dz, 1) * jnp.exp(tops[dz] - highest)
    log_total = jnp.log(summed)
    norm = jnp.where(filled > 0.5, highest + log_total, EMPTY_NORM)

    turned = jnp.zeros((128, 128), F32)
    for p4 in range(16):
        turned = jnp.where(owner == float(4 * p4), norm[p4:p4 + 1, :], turned)
    back = turned[0:32]
    for k in (1, 2, 3):
        back += pltpu.roll(turned[32 * k:32 * k + 32], 128 - 32 * k, 1)
    for d in range(32):
        lt[d, 0:1, :] = back[d:d + 1, :]
    lr[my_u] = lt[my_u]

    def send_norm(t, carry):
        dev, u = plane(t)
        pltpu.make_async_remote_copy(
            src_ref=lt.at[u], dst_ref=lr.at[my_u], send_sem=s_ls, recv_sem=s_lr,
            device_id=dev, device_id_type=MESH,
        ).start()
        return carry

    lax.fori_loop(1, 32, send_norm, 0)

    slot_i = slz[1, 0:1, :].astype(jnp.int32)
    lane_of = ((slot_i // 4) % 4) * 32 + 4 + slot_i % 4
    choose = jnp.where(sub == jnp.broadcast_to(lane_of, (128, 128)), 1.0, 0.0)
    by_lane = jnp.dot(
        log_total, choose, preferred_element_type=F32, precision=lax.Precision.HIGHEST
    )
    p4_row = lax.broadcasted_iota(jnp.int32, (16, 128), 0)
    spread[0:1, :] = jnp.sum(
        jnp.where(p4_row == jnp.broadcast_to(slot_i // 16, (16, 128)), by_lane, 0.0),
        axis=0, keepdims=True,
    )

    pltpu.make_async_copy(lr.at[0:31], lr.at[0:31], s_lr).wait()

    for q in range(4):
        got = jnp.concatenate([lr[8 * q + v, 0:1, :] for v in range(8)], axis=0)
        for j in range(4):
            turn = (32 * (q - j)) % 128
            turned = got if turn == 0 else pltpu.roll(got, turn, 1)
            ss[j] = jnp.where(group == q, turned, ss[j])
    own_col = pl.multiple_of(c * HALF, HALF)
    far_col = pl.multiple_of((1 - c) * HALF, HALF)

    def update(j, carry):
        factor = jnp.exp(ms[j] - ss[j])
        mass = jnp.zeros((BS, 128), F32)
        for n in range(4):
            for h in range(2):
                v = 2 * n + h
                w = e_sc[j, n, :, h * 128:(h + 1) * 128] * factor[v:v + 1, :]
                mass += w
                wb[:, v * 128:(v + 1) * 128] = w.astype(BF16)
        denom = jnp.sum(mass, axis=1, keepdims=True) + LAMBDA
        rows = pl.ds(pl.multiple_of(j * BS, BS), BS)
        at = pl.ds(pl.multiple_of((c * OWN + j) * BS, BS), BS)
        for i, col in ((1, far_col), (0, own_col)):
            sums = jnp.dot(wb[...], inc[j, :, pl.ds(col, HALF)], preferred_element_type=F32)
            prev = ce[rows, pl.ds(col, HALF)].astype(F32)
            fr[i, rows, :] = (sums + LAMBDA * prev) / denom
            if i == 1:
                pltpu.make_async_remote_copy(
                    src_ref=fr.at[1, rows], dst_ref=out.at[at], send_sem=s_fs, recv_sem=s_fr,
                    device_id=(dp, 1 - c), device_id_type=MESH,
                ).start()
            else:
                pltpu.make_async_copy(fr.at[0, rows], out.at[at], s_fl).start()
        return carry

    lax.fori_loop(0, OWN, update, 0)

    pltpu.make_async_copy(fr.at[0], fr.at[0], s_fl).wait()
    pltpu.make_async_copy(fr.at[1], fr.at[1], s_fs).wait()
    pltpu.make_async_copy(fr.at[1], fr.at[1], s_fr).wait()
    for p in range(2):
        pltpu.make_async_copy(raw.at[p, 0, 0:7], raw.at[p, 0, 0:7], s_zs.at[p]).wait()
        pltpu.make_async_copy(raw.at[p, 1:4], raw.at[p, 1:4], s_as.at[p]).wait()
        pltpu.make_async_copy(slp.at[p], slp.at[p], s_slps.at[p]).wait()
        pltpu.make_async_copy(pk.at[p, :, 1:8], pk.at[p, :, 1:8], s_ps.at[p]).wait()
    pltpu.make_async_copy(slz.at[0:7], slz.at[0:7], s_slzs).wait()
    pltpu.make_async_copy(stt.at[0:31], stt.at[0:31], s_sts).wait()
    pltpu.make_async_copy(tz.at[1:8], tz.at[1:8], s_tzs).wait()
    pltpu.make_async_copy(lt.at[0:31], lt.at[0:31], s_ls).wait()


def local(embeddings, parents, block_lists, centroids):
    dma, vmem = pltpu.SemaphoreType.DMA, pltpu.VMEM
    fresh, spread = pl.pallas_call(
        kernel,
        out_shape=(
            jax.ShapeDtypeStruct((2 * OWN * BS, HALF), F32),
            jax.ShapeDtypeStruct((1, ROWS), F32),
        ),
        in_specs=[
            pl.BlockSpec(memory_space=vmem),
            pl.BlockSpec(memory_space=vmem),
            pl.BlockSpec(memory_space=vmem),
            pl.BlockSpec(memory_space=pl.ANY),
        ],
        out_specs=(pl.BlockSpec(memory_space=pl.ANY), pl.BlockSpec(memory_space=vmem)),
        scratch_shapes=[
            vmem((2, 4, 8, ROWS, HALF), BF16),
            vmem((8, 24, 128), F32),
            vmem((2, 3, 8, 8, 128), F32),
            vmem((2, 8, 8, OWN, 16, HALF), BF16),
            vmem((OWN, 1024, D), BF16),
            vmem((OWN * BS, D), BF16),
            vmem((OWN, 4, BS, 256), F32),
            vmem((OWN, 8, 128), F32),
            vmem((OWN, 8, 128), F32),
            vmem((32, 8, 128), F32),
            vmem((32, 8, 128), F32),
            vmem((8, 2, 16, 128), F32),
            vmem((32, 8, 128), F32),
            vmem((32, 8, 128), F32),
            vmem((BS, 1024), BF16),
            vmem((2, OWN * BS, HALF), F32),
            vmem((2, 512, 128), F32),
            vmem((128, 128), F32),
            dma((2,)), dma((2, 8)), dma((2,)), dma((2, 4, 2)),
            dma, dma, dma((2,)), dma((2,)), dma((2,)), dma((2,)), dma((2,)), dma,
            dma, dma, dma, dma, dma, dma, dma, dma, dma,
        ],
        compiler_params=pltpu.CompilerParams(
            collective_id=0, has_side_effects=True, vmem_limit_bytes=56 * 1024 * 1024
        ),
        cost_estimate=pl.CostEstimate(
            flops=8_000_000_000, bytes_accessed=10_000_000, transcendentals=1_000_000
        ),
        name="kmeans_step",
    )(
        embeddings,
        parents.astype(F32).reshape(1, ROWS),
        block_lists.reshape(8, 128),
        centroids,
    )
    return fresh, spread.reshape(ROWS)


def solution(mesh):
    placed = (P(("dp", "rep"), None), P(("dp", "rep")), P(), P("dp", None))
    return jax.shard_map(
        local,
        mesh=mesh,
        in_specs=placed,
        out_specs=(P("dp", "rep"), P(("dp", "rep"))),
        check_vma=False,
    )
```

```python
import math

import jax
import jax.numpy as jnp
from jax import lax
from jax.experimental import pallas as pl
from jax.experimental.pallas import tpu as pltpu
from jax.sharding import PartitionSpec as P

BETA = 3.0
LAMBDA = 0.25
EMPTY_NORM = 1e30
NONE_MAX = -1e30
MESH = pl.DeviceIdType.MESH

NY, NX, NZ, NC = 4, 4, 8, 2
ROWS = 128
D = 1024
HALF = 512
BS = 256
OWN = 4
CAP = 4
ZF = 96
F32 = jnp.float32
BF16 = jnp.bfloat16


def kernel(
    emb, par, bl, cent, out, spread,
    raw, slz, slp, pk, inc, ce, e_sc, ms, ss, stt, rs, tz, lt, lr, wb, fr, keys, pbq,
    s_zs, s_zr, s_as, s_ar, s_bs, s_br, s_ys, s_yr, s_slzs, s_slzr, s_slps, s_slpr, s_ps, s_pr, s_loc, s_ce,
    s_sts, s_str, s_tzs, s_tzr, s_ls, s_lr, s_fs, s_fr,
):
    dp = lax.axis_index("dp")
    c = lax.axis_index("rep")
    y = dp // 32
    x = (dp // 8) % 4
    z = dp % 8

    def chip(yy, xx, zz):
        return (yy * 4 + xx) * 8 + zz

    def zdev(dz):
        return (chip(y, x, (z + dz) % 8), c)

    def adev(p, k, dc=0):
        return (chip((y + k) % 4, x, z) if p == 0 else chip(y, (x + k) % 4, z), c)

    def bdev(p, k, dc):
        cc = (c + dc) % 2
        return (chip(y, (x + k) % 4, z) if p == 0 else chip((y + k) % 4, x, z), cc)

    ys = [(y + t) % 4 for t in range(4)]
    xs = [(x + t) % 4 for t in range(4)]
    cs = [c, 1 - c]

    def plane(t):
        yx = ys[t // 8] * 4 + xs[(t // 2) % 4]
        return (yx * 8 + z, cs[t % 2]), yx * 2 + cs[t % 2]

    my_u = (y * 4 + x) * 2 + c

    ce_copy = pltpu.make_async_copy(cent.at[pl.ds(c * 1024, 1024)], ce, s_ce)
    ce_copy.start()

    barrier = pltpu.get_barrier_semaphore()

    for t in range(1, 32):
        pl.semaphore_signal(barrier, 1, device_id=plane(t)[0], device_id_type=MESH)
    for dz in range(1, 8):
        pl.semaphore_signal(barrier, 1, device_id=zdev(dz), device_id_type=MESH)
    for p in range(2):
        raw[p, 0, 1] = emb[:, p * HALF:(p + 1) * HALF]
    pl.semaphore_wait(barrier, 38)

    def send(src, dst, ssem, rsem, dev):
        pltpu.make_async_remote_copy(
            src_ref=src, dst_ref=dst, send_sem=ssem, recv_sem=rsem,
            device_id=dev, device_id_type=MESH,
        ).start()

    def arrived(ref, sem):
        pltpu.make_async_copy(ref, ref, sem).wait()

    def step_to(pos, step):
        return (pos + 1) % 8 if step < 0 else (pos - 1) % 8

    def zsend(p, pos, step):
        to = step_to(pos, step)
        send(raw.at[p, 0, pos, 0:ZF], raw.at[p, 0, to, 0:ZF], s_zs.at[p], s_zr.at[p, to], zdev(step))

    def zwait(p, pos):
        arrived(raw.at[p, 0, pos, 0:ZF], s_zr.at[p, pos])

    def asend(p, pos):
        for k in (1, 3):
            send(
                raw.at[p, 0, pos, 0:ZF], raw.at[p, 4 - k, pos, 0:ZF],
                s_as.at[p], s_ar.at[p, 4 - k, pos], adev(p, k),
            )

    def afwd(p, pos):
        cut = 48
        for k, lo, hi in ((1, 0, cut), (3, cut, ZF)):
            arrived(raw.at[p, k, pos, 0:ZF], s_ar.at[p, k, pos])
            send(
                raw.at[p, k, pos, lo:hi], raw.at[p, 2, pos, lo:hi],
                s_as.at[p], s_ar.at[p, 2, pos // 4], adev(p, 4 - k),
            )

    def bsend(p):
        for k in (1, 3, 2):
            send(
                raw.at[p, 0, 1, ZF:ROWS], raw.at[p, 4 - k, 1, ZF:ROWS],
                s_bs.at[p], s_br.at[p], adev(p, k),
            )

    def bwait(p):
        arrived(raw.at[p, 1:4, 1, ZF:ROWS], s_br.at[p])

    def ysend(p, pos, step):
        to = step_to(pos, step)
        send(raw.at[p, :, pos, ZF:ROWS], raw.at[p, :, to, ZF:ROWS], s_ys.at[p], s_yr.at[p, to], zdev(step))

    def ywait(p, pos):
        arrived(raw.at[p, :, pos, ZF:ROWS], s_yr.at[p, pos])

    both = range(2)
    for p in both:
        zsend(p, 1, -1)
        zsend(p, 1, 1)
        bsend(p)
        asend(p, 1)

    par_row = par[0:1, :].astype(F32)
    sub = lax.broadcasted_iota(jnp.int32, (ROWS, ROWS), 0)
    lane = lax.broadcasted_iota(jnp.int32, (ROWS, ROWS), 1)
    par_wide = jnp.broadcast_to(par_row, (ROWS, ROWS))
    par_col = jnp.sum(jnp.where(sub == lane, par_wide, 0.0), axis=1, keepdims=True)
    earlier = jnp.where((par_col == par_wide) & (sub < lane), 1.0, 0.0)
    slot_row = par_row * CAP + jnp.sum(earlier, axis=0, keepdims=True)
    slot_col = jnp.sum(
        jnp.where(sub == lane, jnp.broadcast_to(slot_row, (ROWS, ROWS)), 0.0), axis=1, keepdims=True
    )
    slz[1, 0:8, :] = jnp.broadcast_to(slot_row, (8, 128))
    code = ((lane // 32) * CAP + lane % CAP).astype(F32)
    for p4 in range(16):
        hit = jnp.where(slot_col == code + float(16 * p4), 1.0, 0.0)
        slz[1, 8 + p4:9 + p4, :] = jnp.sum(hit, axis=0, keepdims=True)
    for dz in range(1, 8):
        to = (1 - dz) % 8
        pltpu.make_async_remote_copy(
            src_ref=slz.at[1], dst_ref=slz.at[to], send_sem=s_slzs, recv_sem=s_slzr,
            device_id=zdev(dz), device_id_type=MESH,
        ).start()

    lists = jnp.concatenate([bl[0:8, :], bl[8:16, :]], axis=1)

    def lookup(ids):
        n = ids.shape[0]
        which = (lax.broadcasted_iota(jnp.int32, (1, 128), 1) % 64).astype(F32)
        acc = jnp.zeros((n, 128), F32)
        for ch in range(8):
            acc += jnp.where(ids == lists[ch:ch + 1, :], which, 0.0)
        return jnp.sum(acc, axis=1, keepdims=True)

    row = lax.broadcasted_iota(jnp.int32, (512, 1), 0)
    zz = (row // 4) % 4
    core = (row // 64) % 2
    core = jnp.where(core == 0, c, 1 - c)
    for p in range(2):
        far = row // 128
        where_to = chip(y, (x + far) % 4, z) if p == 0 else chip((y + far) % 4, x, z)
        ids = where_to * 8 + core * 4 + (row // 16) % 4
        keys[p] = jnp.broadcast_to(
            lookup(ids) * CAP + (row % 4).astype(F32) + (zz * 256).astype(F32), (512, 128)
        )
    r128 = lax.broadcasted_iota(jnp.int32, (128, 1), 0)
    peer = r128 % 32
    peer_chip = (peer // 2) * 8 + z
    wide = jnp.zeros((128, 128), F32)
    for q in range(4):
        ids = peer_chip * 8 + (peer % 2) * 4 + (q + 4 - r128 // 32) % 4
        wide = jnp.where(lane // 32 == q, lookup(ids) - float(q), wide)
    pbq[...] = wide

    for p in both:
        bwait(p)
        ysend(p, 1, -1)
        ysend(p, 1, 1)
    for p in both:
        zwait(p, 2)
        zsend(p, 2, -1)
        zwait(p, 0)
        zsend(p, 0, 1)
    for p in both:
        asend(p, 2)
        asend(p, 0)
    arrived(slz.at[0:7], s_slzr)
    for p in both:
        for k in (1, 3, 2):
            send(slz.at[:, 0:8, :], slp.at[p, 3 - k], s_slps.at[p], s_slpr.at[p], adev(p, k))
    for p in both:
        afwd(p, 1)
    for p in both:
        zwait(p, 3)
        zsend(p, 3, -1)
        zwait(p, 7)
        zsend(p, 7, 1)
    for p in both:
        asend(p, 3)
        asend(p, 7)
    for p in both:
        afwd(p, 2)
        afwd(p, 0)
    for p in both:
        zwait(p, 4)
        zwait(p, 6)
        zsend(p, 4, -1) if p == 0 else zsend(p, 6, 1)
    for p in both:
        asend(p, 4)
        asend(p, 6)
    for p in both:
        ywait(p, 2)
        ysend(p, 2, -1)
        ywait(p, 0)
        ysend(p, 0, 1)
    for p in both:
        afwd(p, 3)
        afwd(p, 7)
    for p in both:
        zwait(p, 5)
        asend(p, 5)
    for p in both:
        afwd(p, 4)
        afwd(p, 6)
    for p in both:
        ywait(p, 3)
        ysend(p, 3, -1)
        ywait(p, 7)
        ysend(p, 7, 1)
    for p in both:
        arrived(slp.at[p], s_slpr.at[p])

    def pack(p, g, k):
        n = g * 4 + k
        if k == 2:
            arrived(raw.at[p, 2, 4 * g:4 * g + 4, 0:ZF], s_ar.at[p, 2, g])
        key = keys[p][:, 0:1]
        picks = []
        for w in range(4):
            s_row = slz[4 * g + w, 0:1, :] if k == 0 else slp[p, k - 1, 4 * g + w, 0:1, :]
            picks.append(jnp.where(key == s_row + float(256 * w), 1.0, 0.0).astype(BF16))
        pick = jnp.concatenate(picks, axis=1)
        rows = raw[p, k, 4 * g:4 * g + 4].reshape(512, HALF)
        packed = jnp.dot(pick, rows, preferred_element_type=F32).astype(BF16)
        pk[p, n] = packed.reshape(8, OWN, 16, HALF)
        u = (((y + k) % 4) * 4 + x) * 2 + c if p == 0 else (y * 4 + (x + k) % 4) * 2 + c
        off = pl.multiple_of((u % 8) * 128 + (u // 8) * 32 + g * 16, 16)
        dst = inc.at[:, pl.ds(off, 16), p * HALF:(p + 1) * HALF]
        for far in (1, 3, 2, 0):
            for dc in range(2):
                i = far * 2 + dc
                if i == 0:
                    pltpu.make_async_copy(pk.at[p, n, 0], dst, s_loc.at[p]).start()
                else:
                    pltpu.make_async_remote_copy(
                        src_ref=pk.at[p, n, i], dst_ref=dst,
                        send_sem=s_ps.at[p], recv_sem=s_pr.at[p],
                        device_id=bdev(p, far, dc), device_id_type=MESH,
                    ).start()

    for k in (0, 1, 3):
        for p in both:
            pack(p, 0, k)
    for p in both:
        ywait(p, 4)
        ywait(p, 6)
        ysend(p, 4, -1) if p == 0 else ysend(p, 6, 1)
    for p in both:
        pack(p, 0, 2)
    for p in both:
        afwd(p, 5)
    for p in both:
        ywait(p, 5)
    for k in (0, 1, 3, 2):
        for p in both:
            pack(p, 1, k)

    ce_copy.wait()
    for p in range(2):
        got = inc.at[:, 0:896, p * HALF:(p + 1) * HALF]
        pltpu.make_async_copy(got, got, s_pr.at[p]).wait()
        pltpu.make_async_copy(pk.at[p, :, 0], pk.at[p, :, 0], s_loc.at[p]).wait()

    scale = BETA / math.sqrt(D)

    def score(j, carry):
        for n in range(4):
            s = lax.dot_general(
                ce[pl.ds(pl.multiple_of(j * BS, BS), BS), :], inc[j, n * 256:(n + 1) * 256, :],
                (((1,), (1,)), ((), ())), preferred_element_type=F32,
            ) * scale
            top = jnp.max(s, axis=0, keepdims=True)
            e = jnp.exp(s - top)
            e_sc[j, n] = e
            total = jnp.sum(e, axis=0, keepdims=True)
            for h in range(2):
                ms[j, 2 * n + h:2 * n + h + 1, :] = top[:, h * 128:(h + 1) * 128]
                ss[j, 2 * n + h:2 * n + h + 1, :] = total[:, h * 128:(h + 1) * 128]
        return carry

    lax.fori_loop(0, OWN, score, 0)

    group = lax.broadcasted_iota(jnp.int32, (8, 128), 1) // 32
    for q in range(4):
        tops, totals = ms[q], ss[q]
        for j in range(4):
            if j != q:
                turn = (32 * (j - q)) % 128
                tops = jnp.where(group == j, pltpu.roll(ms[j], turn, 1), tops)
                totals = jnp.where(group == j, pltpu.roll(ss[j], turn, 1), totals)
        for v in range(8):
            stt[8 * q + v, 0:1, :] = tops[v:v + 1, :]
            stt[8 * q + v, 1:2, :] = totals[v:v + 1, :]
    rs[my_u] = stt[my_u]

    for t in range(1, 32):
        dev, u = plane(t)
        send(stt.at[u], rs.at[my_u], s_sts, s_str, dev)
    pltpu.make_async_copy(rs.at[0:31], rs.at[0:31], s_str).wait()

    m_in = jnp.concatenate([rs[d, 0:1, :] for d in range(32)], axis=0)
    s_in = jnp.concatenate([rs[d, 1:2, :] for d in range(32)], axis=0)
    m_all = jnp.concatenate([m_in] + [pltpu.roll(m_in, 32 * k, 1) for k in (1, 2, 3)], axis=0)
    s_all = jnp.concatenate([s_in] + [pltpu.roll(s_in, 32 * k, 1) for k in (1, 2, 3)], axis=0)
    owner = pbq[...]
    m_back = jnp.zeros((128, 128), F32)
    for p4 in range(16):
        mine = owner == float(4 * p4)
        top = jnp.max(jnp.where(mine, m_all, NONE_MAX), axis=0, keepdims=True)
        tz[0, 0, p4:p4 + 1, :] = top
        m_back = jnp.where(mine, top, m_back)
    z_all = s_all * jnp.exp(m_all - m_back)
    for p4 in range(16):
        mine = owner == float(4 * p4)
        tz[0, 1, p4:p4 + 1, :] = jnp.sum(jnp.where(mine, z_all, 0.0), axis=0, keepdims=True)

    for dz in range(1, 8):
        pltpu.make_async_remote_copy(
            src_ref=tz.at[0], dst_ref=tz.at[8 - dz], send_sem=s_tzs, recv_sem=s_tzr,
            device_id=zdev(dz), device_id_type=MESH,
        ).start()
    place = lax.broadcasted_iota(jnp.int32, (16, 128), 1) % 32
    filled = jnp.zeros((16, 128), F32)
    for pos in range(8):
        filled = jnp.where(place // 4 == pos, slz[pos, 8:24, :], filled)
    pltpu.make_async_copy(tz.at[1:8], tz.at[1:8], s_tzr).wait()

    def aligned(dz, what):
        t = tz[dz, what]
        if dz == 0:
            return t
        turn = 4 * dz
        return jnp.where(place >= turn, pltpu.roll(t, turn, 1), pltpu.roll(t, 96 + turn, 1))

    tops = [aligned(dz, 0) for dz in range(8)]
    highest = tops[0]
    for t in tops[1:]:
        highest = jnp.maximum(highest, t)
    summed = jnp.zeros((16, 128), F32)
    for dz in range(8):
        summed += aligned(dz, 1) * jnp.exp(tops[dz] - highest)
    log_total = jnp.log(summed)
    norm = jnp.where(filled > 0.5, highest + log_total, EMPTY_NORM)

    turned = jnp.zeros((128, 128), F32)
    for p4 in range(16):
        turned = jnp.where(owner == float(4 * p4), norm[p4:p4 + 1, :], turned)
    back = turned[0:32]
    for k in (1, 2, 3):
        back += pltpu.roll(turned[32 * k:32 * k + 32], 128 - 32 * k, 1)
    for d in range(32):
        lt[d, 0:1, :] = back[d:d + 1, :]
    lr[my_u] = lt[my_u]

    for t in range(1, 32):
        dev, u = plane(t)
        send(lt.at[u], lr.at[my_u], s_ls, s_lr, dev)

    slot_i = slz[1, 0:1, :].astype(jnp.int32)
    lane_of = ((slot_i // 4) % 4) * 32 + 4 + slot_i % 4
    choose = jnp.where(sub == jnp.broadcast_to(lane_of, (128, 128)), 1.0, 0.0)
    by_lane = jnp.dot(
        log_total, choose, preferred_element_type=F32, precision=lax.Precision.HIGHEST
    )
    p4_row = lax.broadcasted_iota(jnp.int32, (16, 128), 0)
    spread[0:1, :] = jnp.sum(
        jnp.where(p4_row == jnp.broadcast_to(slot_i // 16, (16, 128)), by_lane, 0.0),
        axis=0, keepdims=True,
    )

    pltpu.make_async_copy(lr.at[0:31], lr.at[0:31], s_lr).wait()

    for q in range(4):
        got = jnp.concatenate([lr[8 * q + v, 0:1, :] for v in range(8)], axis=0)
        for j in range(4):
            turn = (32 * (q - j)) % 128
            turned = got if turn == 0 else pltpu.roll(got, turn, 1)
            ss[j] = jnp.where(group == q, turned, ss[j])
    own_col = pl.multiple_of(c * HALF, HALF)
    far_col = pl.multiple_of((1 - c) * HALF, HALF)

    def update(j, carry):
        factor = jnp.exp(ms[j] - ss[j])
        mass = jnp.zeros((BS, 128), F32)
        for n in range(4):
            for h in range(2):
                v = 2 * n + h
                w = e_sc[j, n, :, h * 128:(h + 1) * 128] * factor[v:v + 1, :]
                mass += w
                wb[:, v * 128:(v + 1) * 128] = w.astype(BF16)
        denom = jnp.sum(mass, axis=1, keepdims=True) + LAMBDA
        rows = pl.ds(pl.multiple_of(j * BS, BS), BS)
        at = pl.ds(pl.multiple_of((c * OWN + j) * BS, BS), BS)
        for i, col in ((1, far_col), (0, own_col)):
            sums = jnp.dot(wb[...], inc[j, :, pl.ds(col, HALF)], preferred_element_type=F32)
            prev = ce[rows, pl.ds(col, HALF)].astype(F32)
            fresh = (sums + LAMBDA * prev) / denom
            if i == 1:
                fr[rows, :] = fresh
                send(fr.at[rows], out.at[at], s_fs, s_fr, (dp, 1 - c))
            else:
                out[at, :] = fresh
        return carry

    lax.fori_loop(0, OWN, update, 0)

    arrived(fr, s_fs)
    arrived(fr, s_fr)
    for p in both:
        arrived(raw.at[p, 0, 0:7, 0:ZF], s_zs.at[p])
        arrived(raw.at[p, 1:4, :, 0:ZF], s_as.at[p])
        arrived(raw.at[p, 1:4, 1, ZF:ROWS], s_bs.at[p])
        arrived(raw.at[p, :, 0:7, ZF:ROWS], s_ys.at[p])
        arrived(slp.at[p], s_slps.at[p])
        arrived(pk.at[p, :, 1:8], s_ps.at[p])
    pltpu.make_async_copy(slz.at[0:7], slz.at[0:7], s_slzs).wait()
    pltpu.make_async_copy(stt.at[0:31], stt.at[0:31], s_sts).wait()
    pltpu.make_async_copy(tz.at[1:8], tz.at[1:8], s_tzs).wait()
    pltpu.make_async_copy(lt.at[0:31], lt.at[0:31], s_ls).wait()


def local(embeddings, parents, block_lists, centroids):
    dma, vmem = pltpu.SemaphoreType.DMA, pltpu.VMEM
    fresh, spread = pl.pallas_call(
        kernel,
        out_shape=(
            jax.ShapeDtypeStruct((2 * OWN * BS, HALF), F32),
            jax.ShapeDtypeStruct((1, ROWS), F32),
        ),
        in_specs=[
            pl.BlockSpec(memory_space=vmem),
            pl.BlockSpec(memory_space=vmem),
            pl.BlockSpec(memory_space=vmem),
            pl.BlockSpec(memory_space=pl.ANY),
        ],
        out_specs=(pl.BlockSpec(memory_space=vmem), pl.BlockSpec(memory_space=vmem)),
        scratch_shapes=[
            vmem((2, 4, 8, ROWS, HALF), BF16),
            vmem((8, 24, 128), F32),
            vmem((2, 3, 8, 8, 128), F32),
            vmem((2, 8, 8, OWN, 16, HALF), BF16),
            vmem((OWN, 1024, D), BF16),
            vmem((OWN * BS, D), BF16),
            vmem((OWN, 4, BS, 256), F32),
            vmem((OWN, 8, 128), F32),
            vmem((OWN, 8, 128), F32),
            vmem((32, 8, 128), F32),
            vmem((32, 8, 128), F32),
            vmem((8, 2, 16, 128), F32),
            vmem((32, 8, 128), F32),
            vmem((32, 8, 128), F32),
            vmem((BS, 1024), BF16),
            vmem((OWN * BS, HALF), F32),
            vmem((2, 512, 128), F32),
            vmem((128, 128), F32),
            dma((2,)), dma((2, 8)), dma((2,)), dma((2, 4, 8)),
            dma((2,)), dma((2,)), dma((2,)), dma((2, 8)),
            dma, dma, dma((2,)), dma((2,)), dma((2,)), dma((2,)), dma((2,)), dma,
            dma, dma, dma, dma, dma, dma, dma, dma,
        ],
        compiler_params=pltpu.CompilerParams(
            collective_id=0, has_side_effects=True, vmem_limit_bytes=48 * 1024 * 1024
        ),
        cost_estimate=pl.CostEstimate(
            flops=8_000_000_000, bytes_accessed=10_000_000, transcendentals=1_000_000
        ),
        name="kmeans_step",
    )(
        embeddings,
        parents.reshape(1, ROWS),
        block_lists.T,
        centroids,
    )
    return fresh, spread.reshape(ROWS)


def solution(mesh):
    placed = (P(("dp", "rep"), None), P(("dp", "rep")), P(), P("dp", None))
    return jax.shard_map(
        local,
        mesh=mesh,
        in_specs=placed,
        out_specs=(P("dp", "rep"), P(("dp", "rep"))),
        check_vma=False,
    )
```

```python
import math

import jax
import jax.numpy as jnp
from jax import lax
from jax.experimental import pallas as pl
from jax.experimental.pallas import tpu as pltpu
from jax.sharding import PartitionSpec as P

BETA = 3.0
LAMBDA = 0.25
EMPTY_NORM = 1e30
NONE_MAX = -1e30
MESH = pl.DeviceIdType.MESH

NY, NX, NZ, NC = 4, 4, 8, 2
ROWS = 128
D = 1024
HALF = 512
BS = 256
OWN = 4
CAP = 4
ZF = 64
ORDER = (1, 2, 0, 3, 7, 4, 6, 5)
F32 = jnp.float32
BF16 = jnp.bfloat16


def kernel(
    emb, par_in, bl_in, cent, out, spread,
    raw, slz, slp, pk, inc, ce, e_sc, ms, ss, stt, rs, tz, lt, lr, wb, fr, keys, pbq, par, bl,
    s_in, s_zs, s_zr, s_as, s_ar, s_bs, s_br, s_ys, s_yr, s_slzs, s_slzr, s_slps, s_slpr,
    s_ps, s_pr, s_loc, s_ce, s_sts, s_str, s_tzs, s_tzr, s_ls, s_lr, s_fs, s_fr,
):
    dp = lax.axis_index("dp")
    c = lax.axis_index("rep")
    y = dp // 32
    x = (dp // 8) % 4
    z = dp % 8
    first = c == 0
    a_me = jnp.where(first, y, x)
    b_me = jnp.where(first, x, y)
    a_unit = jnp.where(first, 32, 8)
    b_unit = jnp.where(first, 8, 32)

    def zdev(dz):
        return (dp - z + (z + dz) % 8, c)

    def adev(k):
        return (dp + ((a_me + k) % 4 - a_me) * a_unit, c)

    def bdev(k, dc):
        return (dp + ((b_me + k) % 4 - b_me) * b_unit, c if dc == 0 else 1 - c)

    ys = [(y + t) % 4 for t in range(4)]
    xs = [(x + t) % 4 for t in range(4)]

    def plane(t):
        yy, xx = ys[t // 8], xs[(t // 2) % 4]
        cc = c if t % 2 == 0 else 1 - c
        u = jnp.where(cc == 0, xx * 4 + yy, 16 + yy * 4 + xx)
        return ((yy * 4 + xx) * 8 + z, cc), u

    my_u = c * 16 + b_me * 4 + a_me

    def send(src, dst, ssem, rsem, dev):
        pltpu.make_async_remote_copy(
            src_ref=src, dst_ref=dst, send_sem=ssem, recv_sem=rsem,
            device_id=dev, device_id_type=MESH,
        ).start()

    def arrived(ref, sem):
        pltpu.make_async_copy(ref, ref, sem).wait()

    emb_copy = pltpu.make_async_copy(emb, raw.at[1, 0], s_in.at[0])
    par_copy = pltpu.make_async_copy(par_in, par, s_in.at[1])
    bl_copy = pltpu.make_async_copy(bl_in, bl, s_in.at[2])
    ce_copy = pltpu.make_async_copy(cent.at[pl.ds(c * 1024, 1024)], ce, s_ce)
    emb_copy.start()
    par_copy.start()
    bl_copy.start()
    ce_copy.start()

    barrier = pltpu.get_barrier_semaphore()
    for t in range(1, 32):
        pl.semaphore_signal(barrier, 1, device_id=plane(t)[0], device_id_type=MESH)
    for dz in range(1, 8):
        pl.semaphore_signal(barrier, 1, device_id=zdev(dz), device_id_type=MESH)
    emb_copy.wait()
    pl.semaphore_wait(barrier, 38)

    def step_to(pos, step):
        return (pos + 1) % 8 if step < 0 else (pos - 1) % 8

    def zsend(pos, step, lo=0, hi=D):
        to = step_to(pos, step)
        send(
            raw.at[pos, 0, 0:ZF, lo:hi], raw.at[to, 0, 0:ZF, lo:hi],
            s_zs, s_zr.at[to], zdev(step),
        )

    def zwait(pos):
        arrived(raw.at[pos, 0, 0:ZF], s_zr.at[pos])

    def asend(pos):
        for k in (1, 3):
            send(raw.at[pos, 0, 0:ZF], raw.at[pos, 4 - k, 0:ZF], s_as, s_ar.at[4 - k, pos], adev(k))

    def afwd(pos):
        for k, lo, hi in ((1, 0, HALF), (3, HALF, D)):
            arrived(raw.at[pos, k, 0:ZF], s_ar.at[k, pos])
            send(
                raw.at[pos, k, 0:ZF, lo:hi], raw.at[pos, 2, 0:ZF, lo:hi],
                s_as, s_ar.at[2, pos], adev(4 - k),
            )

    def bsend():
        for k in (1, 3, 2):
            send(raw.at[1, 0, ZF:ROWS], raw.at[1, 4 - k, ZF:ROWS], s_bs, s_br, adev(k))

    def bwait():
        arrived(raw.at[1, 1:4, ZF:ROWS], s_br)

    def ysend(pos, step, lo=0, hi=D):
        to = step_to(pos, step)
        send(
            raw.at[pos, :, ZF:ROWS, lo:hi], raw.at[to, :, ZF:ROWS, lo:hi],
            s_ys, s_yr.at[to], zdev(step),
        )

    def ywait(pos):
        arrived(raw.at[pos, :, ZF:ROWS], s_yr.at[pos])

    def pack(pos):
        tau = ORDER.index(pos)
        arrived(raw.at[pos, 2, 0:ZF], s_ar.at[2, pos])
        key = keys[:, 0:1]
        picks = []
        for k in range(4):
            s_row = slz[pos, 0:1, :] if k == 0 else slp[k - 1, pos, 0:1, :]
            picks.append(jnp.where(key == s_row + float(256 * k), 1.0, 0.0).astype(BF16))
        pick = jnp.concatenate(picks, axis=1)
        rows = raw[pos].reshape(512, D)
        packed = jnp.dot(pick, rows, preferred_element_type=F32).astype(BF16)
        pk[tau] = packed.reshape(8, OWN, 16, D)
        off = pl.multiple_of(tau * 128 + c * 64 + b_me * 16, 16)
        dst = inc.at[:, pl.ds(off, 16), :]
        for far in (1, 3, 2, 0):
            for dc in range(2):
                i = far * 2 + dc
                if i == 0:
                    pltpu.make_async_copy(pk.at[tau, 0], dst, s_loc.at[tau]).start()
                else:
                    send(pk.at[tau, i], dst, s_ps, s_pr.at[tau], bdev(far, dc))

    zsend(1, -1)
    zsend(1, 1)
    asend(1)
    bsend()
    zwait(2)
    zsend(2, -1)
    zwait(0)
    zsend(0, 1)
    asend(2)
    afwd(1)
    asend(0)

    par_copy.wait()
    bl_copy.wait()
    par_row = par[0:1, :].astype(F32)
    sub = lax.broadcasted_iota(jnp.int32, (ROWS, ROWS), 0)
    lane = lax.broadcasted_iota(jnp.int32, (ROWS, ROWS), 1)
    par_wide = jnp.broadcast_to(par_row, (ROWS, ROWS))
    par_col = jnp.sum(jnp.where(sub == lane, par_wide, 0.0), axis=1, keepdims=True)
    earlier = jnp.where((par_col == par_wide) & (sub < lane), 1.0, 0.0)
    slot_row = par_row * CAP + jnp.sum(earlier, axis=0, keepdims=True)
    slot_col = jnp.sum(
        jnp.where(sub == lane, jnp.broadcast_to(slot_row, (ROWS, ROWS)), 0.0), axis=1, keepdims=True
    )
    slz[1, 0:8, :] = jnp.broadcast_to(slot_row, (8, 128))
    code = ((lane // 32) * CAP + lane % CAP).astype(F32)
    for p4 in range(16):
        hit = jnp.where(slot_col == code + float(16 * p4), 1.0, 0.0)
        slz[1, 8 + p4:9 + p4, :] = jnp.sum(hit, axis=0, keepdims=True)
    for dz in range(1, 8):
        send(slz.at[1], slz.at[(1 - dz) % 8], s_slzs, s_slzr, zdev(dz))

    bwait()
    zwait(3)
    zsend(3, -1)
    zwait(7)
    zsend(7, 1)
    asend(3)
    arrived(slz.at[0:7], s_slzr)
    for k in (1, 3, 2):
        send(slz.at[:, 0:8, :], slp.at[3 - k], s_slps, s_slpr, adev(k))
    afwd(2)
    ysend(1, -1)
    ysend(1, 1)
    asend(7)

    lists = jnp.concatenate([bl[0:8, :], bl[8:16, :]], axis=1)
    which = (lax.broadcasted_iota(jnp.int32, (1, 128), 1) % 64).astype(F32)

    def lookup(ids):
        acc = jnp.zeros((ids.shape[0], 128), F32)
        for ch in range(8):
            acc += jnp.where(ids == lists[ch:ch + 1, :], which, 0.0)
        return jnp.sum(acc, axis=1, keepdims=True)

    row = lax.broadcasted_iota(jnp.int32, (512, 1), 0)
    far_chip = dp + ((b_me + row // 128) % 4 - b_me) * b_unit
    core = jnp.where((row // 64) % 2 == 0, c, 1 - c)
    word = ((row // 4) % 4 + 4 - a_me) % 4
    keys[...] = jnp.broadcast_to(
        lookup(far_chip * 8 + core * 4 + (row // 16) % 4) * CAP
        + (row % 4).astype(F32) + (word * 256).astype(F32),
        (512, 128),
    )
    r128 = lax.broadcasted_iota(jnp.int32, (128, 1), 0)
    peer = r128 % 32
    high, low = (peer // 4) % 4, peer % 4
    peer_y = jnp.where(peer < 16, low, high)
    peer_x = jnp.where(peer < 16, high, low)
    peer_first = ((peer_y * 4 + peer_x) * 8 + z) * 8 + (peer // 16) * 4
    wide = jnp.zeros((128, 128), F32)
    for q in range(4):
        ids = peer_first + (q + 4 - r128 // 32) % 4
        wide = jnp.where(lane // 32 == q, lookup(ids) - float(q), wide)
    pbq[...] = wide

    zwait(4)
    zsend(4, -1, 0, HALF)
    zwait(6)
    zsend(6, 1, HALF, D)
    asend(6)
    afwd(0)
    asend(4)
    arrived(slp, s_slpr)
    pack(1)
    afwd(3)
    afwd(7)
    afwd(6)
    ywait(2)
    ysend(2, -1)
    ywait(0)
    ysend(0, 1)
    zwait(5)
    asend(5)
    afwd(4)
    pack(0)
    pack(2)
    ywait(3)
    ysend(3, -1)
    ywait(7)
    ysend(7, 1)
    pack(7)
    afwd(5)
    pack(3)
    ywait(4)
    ysend(4, -1, 0, HALF)
    ywait(6)
    ysend(6, 1, HALF, D)
    pack(6)
    pack(4)
    ywait(5)
    pack(5)

    ce_copy.wait()
    scale = BETA / math.sqrt(D)
    for n in range(4):
        for tau in (2 * n, 2 * n + 1):
            arrived(inc.at[:, tau * 128:tau * 128 + 112], s_pr.at[tau])
            arrived(inc.at[:, tau * 128:tau * 128 + 16], s_loc.at[tau])

        def score(j, carry, n=n):
            s = lax.dot_general(
                ce[pl.ds(pl.multiple_of(j * BS, BS), BS), :], inc[j, n * 256:(n + 1) * 256, :],
                (((1,), (1,)), ((), ())), preferred_element_type=F32,
            ) * scale
            top = jnp.max(s, axis=0, keepdims=True)
            e = jnp.exp(s - top)
            e_sc[j, n] = e
            total = jnp.sum(e, axis=0, keepdims=True)
            for h in range(2):
                ms[j, 2 * n + h:2 * n + h + 1, :] = top[:, h * 128:(h + 1) * 128]
                ss[j, 2 * n + h:2 * n + h + 1, :] = total[:, h * 128:(h + 1) * 128]
            return carry

        lax.fori_loop(0, OWN, score, 0)

    sub32 = lax.broadcasted_iota(jnp.int32, (32, 128), 0)
    lane32 = lax.broadcasted_iota(jnp.int32, (32, 128), 1)
    window = ((lane32 + 128 - 4 * sub32) % 128) // 4
    tops = jnp.zeros((32, 128), F32)
    totals = jnp.zeros((32, 128), F32)
    for j in range(OWN):
        for tau, pos in enumerate(ORDER):
            here = window == 8 * j + pos
            turn = 32 * j + 4 * pos
            m_row, s_row = ms[j, tau:tau + 1, :], ss[j, tau:tau + 1, :]
            if turn:
                m_row, s_row = pltpu.roll(m_row, turn, 1), pltpu.roll(s_row, turn, 1)
            tops = jnp.where(here, m_row, tops)
            totals = jnp.where(here, s_row, totals)
    for u in range(32):
        m_row, s_row = tops[u:u + 1, :], totals[u:u + 1, :]
        if u:
            m_row, s_row = pltpu.roll(m_row, 128 - 4 * u, 1), pltpu.roll(s_row, 128 - 4 * u, 1)
        stt[u, 0:1, :] = m_row
        stt[u, 1:2, :] = s_row
    rs[my_u] = stt[my_u]
    for t in range(1, 32):
        dev, u = plane(t)
        send(stt.at[u], rs.at[my_u], s_sts, s_str, dev)
    arrived(rs.at[0:31], s_str)

    m_in = jnp.concatenate([rs[d, 0:1, :] for d in range(32)], axis=0)
    s_in = jnp.concatenate([rs[d, 1:2, :] for d in range(32)], axis=0)
    m_all = jnp.concatenate([m_in] + [pltpu.roll(m_in, 32 * k, 1) for k in (1, 2, 3)], axis=0)
    s_all = jnp.concatenate([s_in] + [pltpu.roll(s_in, 32 * k, 1) for k in (1, 2, 3)], axis=0)
    owner = pbq[...]
    m_back = jnp.zeros((128, 128), F32)
    for p4 in range(16):
        mine = owner == float(4 * p4)
        top = jnp.max(jnp.where(mine, m_all, NONE_MAX), axis=0, keepdims=True)
        tz[0, 0, p4:p4 + 1, :] = top
        m_back = jnp.where(mine, top, m_back)
    z_all = s_all * jnp.exp(m_all - m_back)
    for p4 in range(16):
        mine = owner == float(4 * p4)
        tz[0, 1, p4:p4 + 1, :] = jnp.sum(jnp.where(mine, z_all, 0.0), axis=0, keepdims=True)

    for dz in range(1, 8):
        pltpu.make_async_remote_copy(
            src_ref=tz.at[0], dst_ref=tz.at[8 - dz], send_sem=s_tzs, recv_sem=s_tzr,
            device_id=zdev(dz), device_id_type=MESH,
        ).start()
    place = lax.broadcasted_iota(jnp.int32, (16, 128), 1) % 32
    filled = jnp.zeros((16, 128), F32)
    for pos in range(8):
        filled = jnp.where(place // 4 == pos, slz[pos, 8:24, :], filled)
    pltpu.make_async_copy(tz.at[1:8], tz.at[1:8], s_tzr).wait()

    def aligned(dz, what):
        t = tz[dz, what]
        if dz == 0:
            return t
        turn = 4 * dz
        return jnp.where(place >= turn, pltpu.roll(t, turn, 1), pltpu.roll(t, 96 + turn, 1))

    tops = [aligned(dz, 0) for dz in range(8)]
    highest = tops[0]
    for t in tops[1:]:
        highest = jnp.maximum(highest, t)
    summed = jnp.zeros((16, 128), F32)
    for dz in range(8):
        summed += aligned(dz, 1) * jnp.exp(tops[dz] - highest)
    log_total = jnp.log(summed)
    norm = jnp.where(filled > 0.5, highest + log_total, EMPTY_NORM)

    turned = jnp.zeros((128, 128), F32)
    for p4 in range(16):
        turned = jnp.where(owner == float(4 * p4), norm[p4:p4 + 1, :], turned)
    back = turned[0:32]
    for k in (1, 2, 3):
        back += pltpu.roll(turned[32 * k:32 * k + 32], 128 - 32 * k, 1)
    for d in range(32):
        lt[d, 0:1, :] = back[d:d + 1, :]
    lr[my_u] = lt[my_u]

    for t in range(1, 32):
        dev, u = plane(t)
        send(lt.at[u], lr.at[my_u], s_ls, s_lr, dev)

    slot_i = slz[1, 0:1, :].astype(jnp.int32)
    lane_of = ((slot_i // 4) % 4) * 32 + 4 + slot_i % 4
    choose = jnp.where(sub == jnp.broadcast_to(lane_of, (128, 128)), 1.0, 0.0)
    by_lane = jnp.dot(
        log_total, choose, preferred_element_type=F32, precision=lax.Precision.HIGHEST
    )
    p4_row = lax.broadcasted_iota(jnp.int32, (16, 128), 0)
    spread[0:1, :] = jnp.sum(
        jnp.where(p4_row == jnp.broadcast_to(slot_i // 16, (16, 128)), by_lane, 0.0),
        axis=0, keepdims=True,
    )

    pltpu.make_async_copy(lr.at[0:31], lr.at[0:31], s_lr).wait()

    turned = jnp.concatenate(
        [lr[u, 0:1, :] if u == 0 else pltpu.roll(lr[u, 0:1, :], 4 * u, 1) for u in range(32)], axis=0
    )
    for j in range(OWN):
        for tau, pos in enumerate(ORDER):
            got = jnp.where(window == 8 * j + pos, turned, 0.0)
            got = jnp.sum(got, axis=0, keepdims=True)
            turn = 32 * j + 4 * pos
            ss[j, tau:tau + 1, :] = pltpu.roll(got, 128 - turn, 1) if turn else got
    own_col = pl.multiple_of(c * HALF, HALF)
    far_col = pl.multiple_of((1 - c) * HALF, HALF)

    def update(j, carry):
        factor = jnp.exp(ms[j] - ss[j])
        mass = jnp.zeros((BS, 128), F32)
        for n in range(4):
            for h in range(2):
                v = 2 * n + h
                w = e_sc[j, n, :, h * 128:(h + 1) * 128] * factor[v:v + 1, :]
                mass += w
                wb[:, v * 128:(v + 1) * 128] = w.astype(BF16)
        denom = jnp.sum(mass, axis=1, keepdims=True) + LAMBDA
        rows = pl.ds(pl.multiple_of(j * BS, BS), BS)
        at = pl.ds(pl.multiple_of((c * OWN + j) * BS, BS), BS)
        for i, col in ((1, far_col), (0, own_col)):
            sums = jnp.dot(wb[...], inc[j, :, pl.ds(col, HALF)], preferred_element_type=F32)
            prev = ce[rows, pl.ds(col, HALF)].astype(F32)
            fresh = (sums + LAMBDA * prev) / denom
            if i == 1:
                fr[rows, :] = fresh
                send(fr.at[rows], out.at[at], s_fs, s_fr, (dp, 1 - c))
            else:
                out[at, :] = fresh
        return carry

    lax.fori_loop(0, OWN, update, 0)

    arrived(fr, s_fs)
    arrived(fr, s_fr)
    arrived(raw.at[0:7, 0, 0:ZF], s_zs)
    arrived(raw.at[:, 1:4, 0:ZF], s_as)
    arrived(raw.at[1, 1:4, ZF:ROWS], s_bs)
    arrived(raw.at[0:7, :, ZF:ROWS], s_ys)
    arrived(slz.at[0:7], s_slzs)
    arrived(slp, s_slps)
    arrived(pk.at[:, 1:8], s_ps)
    arrived(stt.at[0:31], s_sts)
    arrived(tz.at[1:8], s_tzs)
    arrived(lt.at[0:31], s_ls)


def local(embeddings, parents, block_lists, centroids):
    dma, vmem = pltpu.SemaphoreType.DMA, pltpu.VMEM
    fresh, spread = pl.pallas_call(
        kernel,
        out_shape=(
            jax.ShapeDtypeStruct((2 * OWN * BS, HALF), F32),
            jax.ShapeDtypeStruct((1, ROWS), F32),
        ),
        in_specs=[pl.BlockSpec(memory_space=pltpu.HBM)] * 4,
        out_specs=(pl.BlockSpec(memory_space=vmem), pl.BlockSpec(memory_space=vmem)),
        scratch_shapes=[
            vmem((8, 4, ROWS, D), BF16),
            vmem((8, 24, 128), F32),
            vmem((3, 8, 8, 128), F32),
            vmem((8, 8, OWN, 16, D), BF16),
            vmem((OWN, 1024, D), BF16),
            vmem((OWN * BS, D), BF16),
            vmem((OWN, 4, BS, 256), F32),
            vmem((OWN, 8, 128), F32),
            vmem((OWN, 8, 128), F32),
            vmem((32, 8, 128), F32),
            vmem((32, 8, 128), F32),
            vmem((8, 2, 16, 128), F32),
            vmem((32, 8, 128), F32),
            vmem((32, 8, 128), F32),
            vmem((BS, 1024), BF16),
            vmem((OWN * BS, HALF), F32),
            vmem((512, 128), F32),
            vmem((128, 128), F32),
            vmem((1, ROWS), jnp.int32),
            vmem((16, 64), jnp.int32),
            dma((3,)), dma, dma((8,)), dma, dma((4, 8)), dma, dma, dma, dma((8,)),
            dma, dma, dma, dma,
            dma, dma((8,)), dma((8,)), dma, dma, dma, dma, dma, dma, dma, dma, dma,
        ],
        compiler_params=pltpu.CompilerParams(
            collective_id=0, has_side_effects=True, vmem_limit_bytes=48 * 1024 * 1024
        ),
        cost_estimate=pl.CostEstimate(
            flops=8_000_000_000, bytes_accessed=10_000_000, transcendentals=1_000_000
        ),
        name="kmeans_step",
    )(
        embeddings,
        parents.reshape(1, ROWS),
        block_lists.T,
        centroids,
    )
    return fresh, spread.reshape(ROWS)


def solution(mesh):
    placed = (P(("dp", "rep"), None), P(("dp", "rep")), P(), P("dp", None))
    return jax.shard_map(
        local,
        mesh=mesh,
        in_specs=placed,
        out_specs=(P("dp", "rep"), P(("dp", "rep"))),
        check_vma=False,
    )
```

```python
import math

import jax
import jax.numpy as jnp
from jax import lax
from jax.experimental import pallas as pl
from jax.experimental.pallas import tpu as pltpu
from jax.sharding import PartitionSpec as P

BETA = 3.0
LAMBDA = 0.25
EMPTY_NORM = 1e30
NONE_MAX = -1e30
MESH = pl.DeviceIdType.MESH

NY, NX, NZ, NC = 4, 4, 8, 2
ROWS = 128
D = 1024
HALF = 512
BS = 256
OWN = 4
CAP = 4
ZF = 64
ORDER = (1, 2, 0, 3, 7, 4, 6, 5)
PLANE = sorted(range(1, 32), key=lambda t: -(min(t // 8, 4 - t // 8) + min(t // 2 % 4, 4 - t // 2 % 4)))
RING = (4, 3, 5, 2, 6, 1, 7)
F32 = jnp.float32
BF16 = jnp.bfloat16


def kernel(
    emb, par_in, bl_in, cent, out, spread,
    raw, slz, slp, pk, inc, ce, e_sc, ms, ss, stt, rs, tz, lt, lr, wb, dn, fr, keys, pbq, par, bl,
    s_in, s_zs, s_zr, s_as, s_ar, s_bs, s_br, s_ys, s_yr, s_slzs, s_slzr, s_slps, s_slpr,
    s_ps, s_pr, s_loc, s_ce, s_sts, s_str, s_tzs, s_tzr, s_ls, s_lr, s_fs, s_fr,
):
    dp = lax.axis_index("dp")
    c = lax.axis_index("rep")
    y = dp // 32
    x = (dp // 8) % 4
    z = dp % 8
    first = c == 0
    a_me = jnp.where(first, y, x)
    b_me = jnp.where(first, x, y)
    a_unit = jnp.where(first, 32, 8)
    b_unit = jnp.where(first, 8, 32)

    def zdev(dz):
        return (dp - z + (z + dz) % 8, c)

    def adev(k):
        return (dp + ((a_me + k) % 4 - a_me) * a_unit, c)

    def bdev(k, dc):
        return (dp + ((b_me + k) % 4 - b_me) * b_unit, c if dc == 0 else 1 - c)

    ys = [(y + t) % 4 for t in range(4)]
    xs = [(x + t) % 4 for t in range(4)]

    def plane(t):
        yy, xx = ys[t // 8], xs[(t // 2) % 4]
        cc = c if t % 2 == 0 else 1 - c
        u = jnp.where(cc == 0, xx * 4 + yy, 16 + yy * 4 + xx)
        return ((yy * 4 + xx) * 8 + z, cc), u

    my_u = c * 16 + b_me * 4 + a_me

    def send(src, dst, ssem, rsem, dev):
        pltpu.make_async_remote_copy(
            src_ref=src, dst_ref=dst, send_sem=ssem, recv_sem=rsem,
            device_id=dev, device_id_type=MESH,
        ).start()

    def arrived(ref, sem):
        pltpu.make_async_copy(ref, ref, sem).wait()

    emb_copy = pltpu.make_async_copy(emb, raw.at[1, 0], s_in.at[0])
    par_copy = pltpu.make_async_copy(par_in, par, s_in.at[1])
    bl_copy = pltpu.make_async_copy(bl_in, bl, s_in.at[2])
    ce_copy = pltpu.make_async_copy(cent.at[pl.ds(c * 1024, 1024)], ce, s_ce)
    emb_copy.start()
    par_copy.start()
    bl_copy.start()
    ce_copy.start()

    barrier = pltpu.get_barrier_semaphore()
    for t in PLANE:
        pl.semaphore_signal(barrier, 1, device_id=plane(t)[0], device_id_type=MESH)
    for dz in RING:
        pl.semaphore_signal(barrier, 1, device_id=zdev(dz), device_id_type=MESH)
    emb_copy.wait()
    pl.semaphore_wait(barrier, 38)

    def step_to(pos, step):
        return (pos + 1) % 8 if step < 0 else (pos - 1) % 8

    def zsend(pos, step, lo=0, hi=D):
        to = step_to(pos, step)
        send(
            raw.at[pos, 0, 0:ZF, lo:hi], raw.at[to, 0, 0:ZF, lo:hi],
            s_zs, s_zr.at[to], zdev(step),
        )

    def zwait(pos):
        arrived(raw.at[pos, 0, 0:ZF], s_zr.at[pos])

    def asend(pos):
        for k in (1, 3):
            send(raw.at[pos, 0, 0:ZF], raw.at[pos, 4 - k, 0:ZF], s_as, s_ar.at[4 - k, pos], adev(k))

    def afwd(pos):
        for k, lo, hi in ((1, 0, HALF), (3, HALF, D)):
            arrived(raw.at[pos, k, 0:ZF], s_ar.at[k, pos])
            send(
                raw.at[pos, k, 0:ZF, lo:hi], raw.at[pos, 2, 0:ZF, lo:hi],
                s_as, s_ar.at[2, pos], adev(4 - k),
            )

    def bsend():
        for k in (1, 3, 2):
            send(raw.at[1, 0, ZF:ROWS], raw.at[1, 4 - k, ZF:ROWS], s_bs, s_br, adev(k))

    def bwait():
        arrived(raw.at[1, 1:4, ZF:ROWS], s_br)

    def ysend(pos, step, lo=0, hi=D):
        to = step_to(pos, step)
        send(
            raw.at[pos, :, ZF:ROWS, lo:hi], raw.at[to, :, ZF:ROWS, lo:hi],
            s_ys, s_yr.at[to], zdev(step),
        )

    def ywait(pos):
        arrived(raw.at[pos, :, ZF:ROWS], s_yr.at[pos])

    def pack(pos):
        tau = ORDER.index(pos)
        arrived(raw.at[pos, 2, 0:ZF], s_ar.at[2, pos])
        key = keys[:, 0:1]
        picks = []
        for k in range(4):
            s_row = slz[pos, 0:1, :] if k == 0 else slp[k - 1, pos, 0:1, :]
            picks.append(jnp.where(key == s_row + float(256 * k), 1.0, 0.0).astype(BF16))
        pick = jnp.concatenate(picks, axis=1)
        rows = raw[pos].reshape(512, D)
        packed = jnp.dot(pick, rows, preferred_element_type=F32).astype(BF16)
        pk[tau] = packed.reshape(8, OWN, 16, D)
        off = pl.multiple_of(tau * 128 + c * 64 + b_me * 16, 16)
        dst = inc.at[:, pl.ds(off, 16), :]
        for far in (1, 3, 2, 0):
            for dc in range(2):
                i = far * 2 + dc
                if i == 0:
                    pltpu.make_async_copy(pk.at[tau, 0], dst, s_loc.at[tau]).start()
                else:
                    send(pk.at[tau, i], dst, s_ps, s_pr.at[tau], bdev(far, dc))

    zsend(1, -1)
    zsend(1, 1)
    asend(1)
    bsend()
    zwait(2)
    zsend(2, -1)
    zwait(0)
    zsend(0, 1)
    asend(2)
    afwd(1)
    asend(0)

    par_copy.wait()
    bl_copy.wait()
    par_row = par[0:1, :].astype(F32)
    sub = lax.broadcasted_iota(jnp.int32, (ROWS, ROWS), 0)
    lane = lax.broadcasted_iota(jnp.int32, (ROWS, ROWS), 1)
    par_wide = jnp.broadcast_to(par_row, (ROWS, ROWS))
    par_col = jnp.sum(jnp.where(sub == lane, par_wide, 0.0), axis=1, keepdims=True)
    earlier = jnp.where((par_col == par_wide) & (sub < lane), 1.0, 0.0)
    slot_row = par_row * CAP + jnp.sum(earlier, axis=0, keepdims=True)
    slot_col = jnp.sum(
        jnp.where(sub == lane, jnp.broadcast_to(slot_row, (ROWS, ROWS)), 0.0), axis=1, keepdims=True
    )
    slz[1, 0:8, :] = jnp.broadcast_to(slot_row, (8, 128))
    code = ((lane // 32) * CAP + lane % CAP).astype(F32)
    for p4 in range(16):
        hit = jnp.where(slot_col == code + float(16 * p4), 1.0, 0.0)
        slz[1, 8 + p4:9 + p4, :] = jnp.sum(hit, axis=0, keepdims=True)
    for dz in RING:
        send(slz.at[1], slz.at[(1 - dz) % 8], s_slzs, s_slzr, zdev(dz))

    bwait()
    zwait(3)
    zsend(3, -1)
    zwait(7)
    zsend(7, 1)
    asend(3)
    arrived(slz.at[0:7], s_slzr)
    for k in (1, 3, 2):
        send(slz.at[:, 0:8, :], slp.at[3 - k], s_slps, s_slpr, adev(k))
    afwd(2)
    ysend(1, -1)
    ysend(1, 1)
    asend(7)

    lists = jnp.concatenate([bl[0:8, :], bl[8:16, :]], axis=1)
    which = (lax.broadcasted_iota(jnp.int32, (1, 128), 1) % 64).astype(F32)

    def lookup(ids):
        acc = jnp.zeros((ids.shape[0], 128), F32)
        for ch in range(8):
            acc += jnp.where(ids == lists[ch:ch + 1, :], which, 0.0)
        return jnp.sum(acc, axis=1, keepdims=True)

    row = lax.broadcasted_iota(jnp.int32, (512, 1), 0)
    far_chip = dp + ((b_me + row // 128) % 4 - b_me) * b_unit
    core = jnp.where((row // 64) % 2 == 0, c, 1 - c)
    word = ((row // 4) % 4 + 4 - a_me) % 4
    keys[...] = jnp.broadcast_to(
        lookup(far_chip * 8 + core * 4 + (row // 16) % 4) * CAP
        + (row % 4).astype(F32) + (word * 256).astype(F32),
        (512, 128),
    )
    r128 = lax.broadcasted_iota(jnp.int32, (128, 1), 0)
    peer = r128 % 32
    high, low = (peer // 4) % 4, peer % 4
    peer_y = jnp.where(peer < 16, low, high)
    peer_x = jnp.where(peer < 16, high, low)
    peer_first = ((peer_y * 4 + peer_x) * 8 + z) * 8 + (peer // 16) * 4
    wide = jnp.zeros((128, 128), F32)
    for q in range(4):
        ids = peer_first + (q + 4 - r128 // 32) % 4
        wide = jnp.where(lane // 32 == q, lookup(ids) - float(q), wide)
    pbq[...] = wide

    zwait(4)
    zsend(4, -1, 0, HALF)
    zwait(6)
    zsend(6, 1, HALF, D)
    asend(6)
    afwd(0)
    asend(4)
    arrived(slp, s_slpr)
    pack(1)
    afwd(3)
    afwd(7)
    afwd(6)
    ywait(2)
    ysend(2, -1)
    ywait(0)
    ysend(0, 1)
    zwait(5)
    asend(5)
    afwd(4)
    pack(0)
    pack(2)
    ywait(3)
    ysend(3, -1)
    ywait(7)
    ysend(7, 1)
    pack(7)
    afwd(5)
    pack(3)
    ywait(4)
    ysend(4, -1, 0, HALF)
    ywait(6)
    ysend(6, 1, HALF, D)
    pack(6)
    pack(4)
    ywait(5)
    pack(5)

    ce_copy.wait()
    scale = BETA / math.sqrt(D)
    for n in range(4):
        for tau in (2 * n, 2 * n + 1):
            arrived(inc.at[:, tau * 128:tau * 128 + 112], s_pr.at[tau])
            arrived(inc.at[:, tau * 128:tau * 128 + 16], s_loc.at[tau])

        def score(j, carry, n=n):
            s = lax.dot_general(
                ce[pl.ds(pl.multiple_of(j * BS, BS), BS), :], inc[j, n * 256:(n + 1) * 256, :],
                (((1,), (1,)), ((), ())), preferred_element_type=F32,
            ) * scale
            top = jnp.max(s, axis=0, keepdims=True)
            e = jnp.exp(s - top)
            e_sc[j, n] = e
            total = jnp.sum(e, axis=0, keepdims=True)
            for h in range(2):
                ms[j, 2 * n + h:2 * n + h + 1, :] = top[:, h * 128:(h + 1) * 128]
                ss[j, 2 * n + h:2 * n + h + 1, :] = total[:, h * 128:(h + 1) * 128]
            return carry

        lax.fori_loop(0, OWN, score, 0)

    sub32 = lax.broadcasted_iota(jnp.int32, (32, 128), 0)
    lane32 = lax.broadcasted_iota(jnp.int32, (32, 128), 1)
    window = ((lane32 + 128 - 4 * sub32) % 128) // 4
    tops = jnp.zeros((32, 128), F32)
    totals = jnp.zeros((32, 128), F32)
    for j in range(OWN):
        for tau, pos in enumerate(ORDER):
            here = window == 8 * j + pos
            turn = 32 * j + 4 * pos
            m_row, s_row = ms[j, tau:tau + 1, :], ss[j, tau:tau + 1, :]
            if turn:
                m_row, s_row = pltpu.roll(m_row, turn, 1), pltpu.roll(s_row, turn, 1)
            tops = jnp.where(here, m_row, tops)
            totals = jnp.where(here, s_row, totals)
    for u in range(32):
        m_row, s_row = tops[u:u + 1, :], totals[u:u + 1, :]
        if u:
            m_row, s_row = pltpu.roll(m_row, 128 - 4 * u, 1), pltpu.roll(s_row, 128 - 4 * u, 1)
        stt[u, 0:1, :] = m_row
        stt[u, 1:2, :] = s_row
    rs[my_u] = stt[my_u]
    for t in PLANE:
        dev, u = plane(t)
        send(stt.at[u], rs.at[my_u], s_sts, s_str, dev)
    arrived(rs.at[0:31], s_str)

    m_in = jnp.concatenate([rs[d, 0:1, :] for d in range(32)], axis=0)
    s_in = jnp.concatenate([rs[d, 1:2, :] for d in range(32)], axis=0)
    m_all = jnp.concatenate([m_in] + [pltpu.roll(m_in, 32 * k, 1) for k in (1, 2, 3)], axis=0)
    s_all = jnp.concatenate([s_in] + [pltpu.roll(s_in, 32 * k, 1) for k in (1, 2, 3)], axis=0)
    owner = pbq[...]
    m_back = jnp.zeros((128, 128), F32)
    for p4 in range(16):
        mine = owner == float(4 * p4)
        top = jnp.max(jnp.where(mine, m_all, NONE_MAX), axis=0, keepdims=True)
        tz[0, 0, p4:p4 + 1, :] = top
        m_back = jnp.where(mine, top, m_back)
    z_all = s_all * jnp.exp(m_all - m_back)
    for p4 in range(16):
        mine = owner == float(4 * p4)
        tz[0, 1, p4:p4 + 1, :] = jnp.sum(jnp.where(mine, z_all, 0.0), axis=0, keepdims=True)

    for dz in RING:
        pltpu.make_async_remote_copy(
            src_ref=tz.at[0], dst_ref=tz.at[8 - dz], send_sem=s_tzs, recv_sem=s_tzr,
            device_id=zdev(dz), device_id_type=MESH,
        ).start()
    place = lax.broadcasted_iota(jnp.int32, (16, 128), 1) % 32
    filled = jnp.zeros((16, 128), F32)
    for pos in range(8):
        filled = jnp.where(place // 4 == pos, slz[pos, 8:24, :], filled)
    pltpu.make_async_copy(tz.at[1:8], tz.at[1:8], s_tzr).wait()

    def aligned(dz, what):
        t = tz[dz, what]
        if dz == 0:
            return t
        turn = 4 * dz
        return jnp.where(place >= turn, pltpu.roll(t, turn, 1), pltpu.roll(t, 96 + turn, 1))

    tops = [aligned(dz, 0) for dz in range(8)]
    highest = tops[0]
    for t in tops[1:]:
        highest = jnp.maximum(highest, t)
    summed = jnp.zeros((16, 128), F32)
    for dz in range(8):
        summed += aligned(dz, 1) * jnp.exp(tops[dz] - highest)
    log_total = jnp.log(summed)
    norm = jnp.where(filled > 0.5, highest + log_total, EMPTY_NORM)

    turned = jnp.zeros((128, 128), F32)
    for p4 in range(16):
        turned = jnp.where(owner == float(4 * p4), norm[p4:p4 + 1, :], turned)
    back = turned[0:32]
    for k in (1, 2, 3):
        back += pltpu.roll(turned[32 * k:32 * k + 32], 128 - 32 * k, 1)
    for d in range(32):
        lt[d, 0:1, :] = back[d:d + 1, :]
    lr[my_u] = lt[my_u]

    for t in PLANE:
        dev, u = plane(t)
        send(lt.at[u], lr.at[my_u], s_ls, s_lr, dev)

    slot_i = slz[1, 0:1, :].astype(jnp.int32)
    lane_of = ((slot_i // 4) % 4) * 32 + 4 + slot_i % 4
    choose = jnp.where(sub == jnp.broadcast_to(lane_of, (128, 128)), 1.0, 0.0)
    by_lane = jnp.dot(
        log_total, choose, preferred_element_type=F32, precision=lax.Precision.HIGHEST
    )
    p4_row = lax.broadcasted_iota(jnp.int32, (16, 128), 0)
    spread[0:1, :] = jnp.sum(
        jnp.where(p4_row == jnp.broadcast_to(slot_i // 16, (16, 128)), by_lane, 0.0),
        axis=0, keepdims=True,
    )

    pltpu.make_async_copy(lr.at[0:31], lr.at[0:31], s_lr).wait()

    turned = jnp.concatenate(
        [lr[u, 0:1, :] if u == 0 else pltpu.roll(lr[u, 0:1, :], 4 * u, 1) for u in range(32)], axis=0
    )
    for j in range(OWN):
        for tau, pos in enumerate(ORDER):
            got = jnp.where(window == 8 * j + pos, turned, 0.0)
            got = jnp.sum(got, axis=0, keepdims=True)
            turn = 32 * j + 4 * pos
            ss[j, tau:tau + 1, :] = pltpu.roll(got, 128 - turn, 1) if turn else got
    own_col = pl.multiple_of(c * HALF, HALF)
    far_col = pl.multiple_of((1 - c) * HALF, HALF)

    def update(j, carry):
        factor = jnp.exp(ms[j] - ss[j])
        mass = jnp.zeros((BS, 128), F32)
        for n in range(4):
            for h in range(2):
                v = 2 * n + h
                w = e_sc[j, n, :, h * 128:(h + 1) * 128] * factor[v:v + 1, :]
                mass += w
                wb[j, :, v * 128:(v + 1) * 128] = w.astype(BF16)
        denom = jnp.sum(mass, axis=1, keepdims=True) + LAMBDA
        rows = pl.ds(pl.multiple_of(j * BS, BS), BS)
        dn[rows, :] = jnp.broadcast_to(denom, (BS, 128))
        sums = jnp.dot(wb[j], inc[j, :, pl.ds(far_col, HALF)], preferred_element_type=F32)
        prev = ce[rows, pl.ds(far_col, HALF)].astype(F32)
        fr[rows, :] = (sums + LAMBDA * prev) / denom
        at = pl.ds(pl.multiple_of((c * OWN + j) * BS, BS), BS)
        send(fr.at[rows], out.at[at], s_fs, s_fr, (dp, 1 - c))
        return carry

    def update_own(j, carry):
        rows = pl.ds(pl.multiple_of(j * BS, BS), BS)
        at = pl.ds(pl.multiple_of((c * OWN + j) * BS, BS), BS)
        sums = jnp.dot(wb[j], inc[j, :, pl.ds(own_col, HALF)], preferred_element_type=F32)
        prev = ce[rows, pl.ds(own_col, HALF)].astype(F32)
        out[at, :] = (sums + LAMBDA * prev) / dn[rows, 0:1]
        return carry

    lax.fori_loop(0, OWN, update, 0)
    lax.fori_loop(0, OWN, update_own, 0)

    arrived(fr, s_fs)
    arrived(fr, s_fr)
    arrived(raw.at[0:7, 0, 0:ZF], s_zs)
    arrived(raw.at[:, 1:4, 0:ZF], s_as)
    arrived(raw.at[1, 1:4, ZF:ROWS], s_bs)
    arrived(raw.at[0:7, :, ZF:ROWS], s_ys)
    arrived(slz.at[0:7], s_slzs)
    arrived(slp, s_slps)
    arrived(pk.at[:, 1:8], s_ps)
    arrived(stt.at[0:31], s_sts)
    arrived(tz.at[1:8], s_tzs)
    arrived(lt.at[0:31], s_ls)


def local(embeddings, parents, block_lists, centroids):
    dma, vmem = pltpu.SemaphoreType.DMA, pltpu.VMEM
    fresh, spread = pl.pallas_call(
        kernel,
        out_shape=(
            jax.ShapeDtypeStruct((2 * OWN * BS, HALF), F32),
            jax.ShapeDtypeStruct((1, ROWS), F32),
        ),
        in_specs=[pl.BlockSpec(memory_space=pltpu.HBM)] * 4,
        out_specs=(pl.BlockSpec(memory_space=vmem), pl.BlockSpec(memory_space=vmem)),
        scratch_shapes=[
            vmem((8, 4, ROWS, D), BF16),
            vmem((8, 24, 128), F32),
            vmem((3, 8, 8, 128), F32),
            vmem((8, 8, OWN, 16, D), BF16),
            vmem((OWN, 1024, D), BF16),
            vmem((OWN * BS, D), BF16),
            vmem((OWN, 4, BS, 256), F32),
            vmem((OWN, 8, 128), F32),
            vmem((OWN, 8, 128), F32),
            vmem((32, 8, 128), F32),
            vmem((32, 8, 128), F32),
            vmem((8, 2, 16, 128), F32),
            vmem((32, 8, 128), F32),
            vmem((32, 8, 128), F32),
            vmem((OWN, BS, 1024), BF16),
            vmem((OWN * BS, 128), F32),
            vmem((OWN * BS, HALF), F32),
            vmem((512, 128), F32),
            vmem((128, 128), F32),
            vmem((1, ROWS), jnp.int32),
            vmem((16, 64), jnp.int32),
            dma((3,)), dma, dma((8,)), dma, dma((4, 8)), dma, dma, dma, dma((8,)),
            dma, dma, dma, dma,
            dma, dma((8,)), dma((8,)), dma, dma, dma, dma, dma, dma, dma, dma, dma,
        ],
        compiler_params=pltpu.CompilerParams(
            collective_id=0, has_side_effects=True, vmem_limit_bytes=48 * 1024 * 1024
        ),
        cost_estimate=pl.CostEstimate(
            flops=8_000_000_000, bytes_accessed=10_000_000, transcendentals=1_000_000
        ),
        name="kmeans_step",
    )(
        embeddings,
        parents.reshape(1, ROWS),
        block_lists.T,
        centroids,
    )
    return fresh, spread.reshape(ROWS)


def solution(mesh):
    placed = (P(("dp", "rep"), None), P(("dp", "rep")), P(), P("dp", None))
    return jax.shard_map(
        local,
        mesh=mesh,
        in_specs=placed,
        out_specs=(P("dp", "rep"), P(("dp", "rep"))),
        check_vma=False,
    )
```

```python
import math

import jax
import jax.numpy as jnp
from jax import lax
from jax.experimental import pallas as pl
from jax.experimental.pallas import tpu as pltpu
from jax.sharding import PartitionSpec as P

BETA = 3.0
LAMBDA = 0.25
EMPTY_NORM = 1e30
NONE_MAX = -1e30
MESH = pl.DeviceIdType.MESH

NY, NX, NZ, NC = 4, 4, 8, 2
ROWS = 128
D = 1024
HALF = 512
BS = 256
OWN = 4
CAP = 4
ZF = 64
ORDER = (1, 2, 0, 3, 7, 4, 6, 5)
PLANE = sorted(range(1, 32), key=lambda t: -(min(t // 8, 4 - t // 8) + min(t // 2 % 4, 4 - t // 2 % 4)))
RING = (4, 3, 5, 2, 6, 1, 7)
F32 = jnp.float32
BF16 = jnp.bfloat16


def kernel(
    emb, par_in, bl_in, cent, out, spread,
    raw, slz, slp, pk, inc, ce, e_sc, ms, ss, stt, rs, tz, lt, lr, wb, dn, fr, keys, pbq, par, bl,
    s_in, s_zs, s_zr, s_as, s_ar, s_bs, s_br, s_ys, s_yr, s_slzs, s_slzr, s_slps, s_slpr,
    s_ps, s_pr, s_loc, s_ce, s_sts, s_str, s_tzs, s_tzr, s_ls, s_lr, s_fs, s_fr,
):
    dp = lax.axis_index("dp")
    c = lax.axis_index("rep")
    y = dp // 32
    x = (dp // 8) % 4
    z = dp % 8
    first = c == 0
    a_me = jnp.where(first, y, x)
    b_me = jnp.where(first, x, y)
    a_unit = jnp.where(first, 32, 8)
    b_unit = jnp.where(first, 8, 32)

    def zdev(dz):
        return (dp - z + (z + dz) % 8, c)

    def adev(k):
        return (dp + ((a_me + k) % 4 - a_me) * a_unit, c)

    def bdev(k, dc):
        return (dp + ((b_me + k) % 4 - b_me) * b_unit, c if dc == 0 else 1 - c)

    ys = [(y + t) % 4 for t in range(4)]
    xs = [(x + t) % 4 for t in range(4)]

    def plane(t):
        yy, xx = ys[t // 8], xs[(t // 2) % 4]
        cc = c if t % 2 == 0 else 1 - c
        u = jnp.where(cc == 0, xx * 4 + yy, 16 + yy * 4 + xx)
        return ((yy * 4 + xx) * 8 + z, cc), u

    my_u = c * 16 + b_me * 4 + a_me

    def send(src, dst, ssem, rsem, dev):
        pltpu.make_async_remote_copy(
            src_ref=src, dst_ref=dst, send_sem=ssem, recv_sem=rsem,
            device_id=dev, device_id_type=MESH,
        ).start()

    def arrived(ref, sem):
        pltpu.make_async_copy(ref, ref, sem).wait()

    emb_copy = pltpu.make_async_copy(emb, raw.at[1, 0], s_in.at[0])
    par_copy = pltpu.make_async_copy(par_in, par, s_in.at[1])
    bl_copy = pltpu.make_async_copy(bl_in, bl, s_in.at[2])
    ce_copy = pltpu.make_async_copy(cent.at[pl.ds(c * 1024, 1024)], ce, s_ce)
    emb_copy.start()
    par_copy.start()
    bl_copy.start()
    ce_copy.start()

    barrier = pltpu.get_barrier_semaphore()
    for t in PLANE:
        pl.semaphore_signal(barrier, 1, device_id=plane(t)[0], device_id_type=MESH)
    for dz in RING:
        pl.semaphore_signal(barrier, 1, device_id=zdev(dz), device_id_type=MESH)
    emb_copy.wait()
    pl.semaphore_wait(barrier, 38)

    def step_to(pos, step):
        return (pos + 1) % 8 if step < 0 else (pos - 1) % 8

    def zsend(pos, step, lo=0, hi=D):
        to = step_to(pos, step)
        send(
            raw.at[pos, 0, 0:ZF, lo:hi], raw.at[to, 0, 0:ZF, lo:hi],
            s_zs, s_zr.at[to], zdev(step),
        )

    def zwait(pos):
        arrived(raw.at[pos, 0, 0:ZF], s_zr.at[pos])

    def asend(pos):
        for k in (1, 3):
            send(raw.at[pos, 0, 0:ZF], raw.at[pos, 4 - k, 0:ZF], s_as, s_ar.at[4 - k, pos], adev(k))

    def afwd(pos):
        for k, lo, hi in ((1, 0, HALF), (3, HALF, D)):
            arrived(raw.at[pos, k, 0:ZF], s_ar.at[k, pos])
            send(
                raw.at[pos, k, 0:ZF, lo:hi], raw.at[pos, 2, 0:ZF, lo:hi],
                s_as, s_ar.at[2, pos], adev(4 - k),
            )

    def bsend():
        for k in (1, 3, 2):
            send(raw.at[1, 0, ZF:ROWS], raw.at[1, 4 - k, ZF:ROWS], s_bs, s_br, adev(k))

    def bwait():
        arrived(raw.at[1, 1:4, ZF:ROWS], s_br)

    def ysend(pos, step, lo=0, hi=D):
        to = step_to(pos, step)
        send(
            raw.at[pos, :, ZF:ROWS, lo:hi], raw.at[to, :, ZF:ROWS, lo:hi],
            s_ys, s_yr.at[to], zdev(step),
        )

    def ywait(pos):
        arrived(raw.at[pos, :, ZF:ROWS], s_yr.at[pos])

    def pack(pos):
        tau = ORDER.index(pos)
        arrived(raw.at[pos, 2, 0:ZF], s_ar.at[2, pos])
        key = keys[:, 0:1]
        picks = []
        for k in range(4):
            s_row = slz[pos, 0:1, :] if k == 0 else slp[k - 1, pos, 0:1, :]
            picks.append(jnp.where(key == s_row + float(256 * k), 1.0, 0.0).astype(BF16))
        pick = jnp.concatenate(picks, axis=1)
        rows = raw[pos].reshape(512, D)
        packed = jnp.dot(pick, rows, preferred_element_type=F32).astype(BF16)
        pk[tau] = packed.reshape(8, OWN, 16, D)
        off = pl.multiple_of(tau * 128 + c * 64 + b_me * 16, 16)
        dst = inc.at[:, pl.ds(off, 16), :]
        for far in (1, 3, 2, 0):
            for dc in range(2):
                i = far * 2 + dc
                if i == 0:
                    pltpu.make_async_copy(pk.at[tau, 0], dst, s_loc.at[tau]).start()
                else:
                    send(pk.at[tau, i], dst, s_ps, s_pr.at[tau], bdev(far, dc))

    zsend(1, -1)
    zsend(1, 1)
    asend(1)
    bsend()
    zwait(2)
    zsend(2, -1)
    zwait(0)
    zsend(0, 1)
    asend(2)
    afwd(1)
    asend(0)

    par_copy.wait()
    bl_copy.wait()
    par_row = par[0:1, :].astype(F32)
    sub = lax.broadcasted_iota(jnp.int32, (ROWS, ROWS), 0)
    lane = lax.broadcasted_iota(jnp.int32, (ROWS, ROWS), 1)
    par_wide = jnp.broadcast_to(par_row, (ROWS, ROWS))
    par_col = jnp.sum(jnp.where(sub == lane, par_wide, 0.0), axis=1, keepdims=True)
    earlier = jnp.where((par_col == par_wide) & (sub < lane), 1.0, 0.0)
    slot_row = par_row * CAP + jnp.sum(earlier, axis=0, keepdims=True)
    slot_col = jnp.sum(
        jnp.where(sub == lane, jnp.broadcast_to(slot_row, (ROWS, ROWS)), 0.0), axis=1, keepdims=True
    )
    slz[1, 0:8, :] = jnp.broadcast_to(slot_row, (8, 128))
    code = ((lane // 32) * CAP + lane % CAP).astype(F32)
    for p4 in range(16):
        hit = jnp.where(slot_col == code + float(16 * p4), 1.0, 0.0)
        slz[1, 8 + p4:9 + p4, :] = jnp.sum(hit, axis=0, keepdims=True)
    for dz in RING:
        send(slz.at[1], slz.at[(1 - dz) % 8], s_slzs, s_slzr, zdev(dz))

    bwait()
    zwait(3)
    zsend(3, -1)
    zwait(7)
    zsend(7, 1)
    asend(3)
    arrived(slz.at[0:7], s_slzr)
    for k in (1, 3, 2):
        send(slz.at[:, 0:8, :], slp.at[3 - k], s_slps, s_slpr, adev(k))
    afwd(2)
    ysend(1, -1)
    ysend(1, 1)
    asend(7)

    lists = jnp.concatenate([bl[0:8, :], bl[8:16, :]], axis=1)
    which = (lax.broadcasted_iota(jnp.int32, (1, 128), 1) % 64).astype(F32)

    def lookup(ids):
        acc = jnp.zeros((ids.shape[0], 128), F32)
        for ch in range(8):
            acc += jnp.where(ids == lists[ch:ch + 1, :], which, 0.0)
        return jnp.sum(acc, axis=1, keepdims=True)

    row = lax.broadcasted_iota(jnp.int32, (512, 1), 0)
    far_chip = dp + ((b_me + row // 128) % 4 - b_me) * b_unit
    core = jnp.where((row // 64) % 2 == 0, c, 1 - c)
    word = ((row // 4) % 4 + 4 - a_me) % 4
    keys[...] = jnp.broadcast_to(
        lookup(far_chip * 8 + core * 4 + (row // 16) % 4) * CAP
        + (row % 4).astype(F32) + (word * 256).astype(F32),
        (512, 128),
    )
    r128 = lax.broadcasted_iota(jnp.int32, (128, 1), 0)
    peer = r128 % 32
    high, low = (peer // 4) % 4, peer % 4
    peer_y = jnp.where(peer < 16, low, high)
    peer_x = jnp.where(peer < 16, high, low)
    peer_first = ((peer_y * 4 + peer_x) * 8 + z) * 8 + (peer // 16) * 4
    wide = jnp.zeros((128, 128), F32)
    for q in range(4):
        ids = peer_first + (q + 4 - r128 // 32) % 4
        wide = jnp.where(lane // 32 == q, lookup(ids) - float(q), wide)
    pbq[...] = wide

    zwait(4)
    zsend(4, -1, 0, HALF)
    zwait(6)
    zsend(6, 1, HALF, D)
    asend(6)
    afwd(0)
    asend(4)
    arrived(slp, s_slpr)
    pack(1)
    afwd(3)
    afwd(7)
    afwd(6)
    ywait(2)
    ysend(2, -1)
    ywait(0)
    ysend(0, 1)
    zwait(5)
    asend(5)
    afwd(4)
    pack(0)
    pack(2)
    ywait(3)
    ysend(3, -1)
    ywait(7)
    ysend(7, 1)
    pack(7)
    afwd(5)
    pack(3)
    ywait(4)
    ysend(4, -1, 0, HALF)
    ywait(6)
    ysend(6, 1, HALF, D)
    pack(6)
    pack(4)
    ywait(5)
    pack(5)

    ce_copy.wait()
    scale = BETA / math.sqrt(D)
    sub32 = lax.broadcasted_iota(jnp.int32, (32, 128), 0)
    lane32 = lax.broadcasted_iota(jnp.int32, (32, 128), 1)
    window = ((lane32 + 128 - 4 * sub32) % 128) // 4
    tops = jnp.zeros((32, 128), F32)
    totals = jnp.zeros((32, 128), F32)
    for taus in ((0, 1), (2, 3), (4, 5), (6,), (7,)):
        for tau in taus:
            arrived(inc.at[:, tau * 128:tau * 128 + 112], s_pr.at[tau])
            arrived(inc.at[:, tau * 128:tau * 128 + 16], s_loc.at[tau])

        def score(j, carry, taus=taus):
            lo, width = taus[0] * 128, len(taus) * 128
            s = lax.dot_general(
                ce[pl.ds(pl.multiple_of(j * BS, BS), BS), :], inc[j, lo:lo + width, :],
                (((1,), (1,)), ((), ())), preferred_element_type=F32,
            ) * scale
            top = jnp.max(s, axis=0, keepdims=True)
            e = jnp.exp(s - top)
            e_sc[j, lo // 256, :, lo % 256:lo % 256 + width] = e
            total = jnp.sum(e, axis=0, keepdims=True)
            for h, tau in enumerate(taus):
                ms[j, tau:tau + 1, :] = top[:, h * 128:(h + 1) * 128]
                ss[j, tau:tau + 1, :] = total[:, h * 128:(h + 1) * 128]
            return carry

        lax.fori_loop(0, OWN, score, 0)
        for j in range(OWN):
            for tau in taus:
                here = window == 8 * j + ORDER[tau]
                turn = 32 * j + 4 * ORDER[tau]
                m_row, s_row = ms[j, tau:tau + 1, :], ss[j, tau:tau + 1, :]
                if turn:
                    m_row, s_row = pltpu.roll(m_row, turn, 1), pltpu.roll(s_row, turn, 1)
                tops = jnp.where(here, m_row, tops)
                totals = jnp.where(here, s_row, totals)

    for u in range(32):
        m_row, s_row = tops[u:u + 1, :], totals[u:u + 1, :]
        if u:
            m_row, s_row = pltpu.roll(m_row, 128 - 4 * u, 1), pltpu.roll(s_row, 128 - 4 * u, 1)
        stt[u, 0:1, :] = m_row
        stt[u, 1:2, :] = s_row
    rs[my_u] = stt[my_u]
    for t in PLANE:
        dev, u = plane(t)
        send(stt.at[u], rs.at[my_u], s_sts, s_str, dev)
    arrived(rs.at[0:31], s_str)

    m_in = jnp.concatenate([rs[d, 0:1, :] for d in range(32)], axis=0)
    s_in = jnp.concatenate([rs[d, 1:2, :] for d in range(32)], axis=0)
    m_all = jnp.concatenate([m_in] + [pltpu.roll(m_in, 32 * k, 1) for k in (1, 2, 3)], axis=0)
    s_all = jnp.concatenate([s_in] + [pltpu.roll(s_in, 32 * k, 1) for k in (1, 2, 3)], axis=0)
    owner = pbq[...]
    m_back = jnp.zeros((128, 128), F32)
    for p4 in range(16):
        mine = owner == float(4 * p4)
        top = jnp.max(jnp.where(mine, m_all, NONE_MAX), axis=0, keepdims=True)
        tz[0, 0, p4:p4 + 1, :] = top
        m_back = jnp.where(mine, top, m_back)
    z_all = s_all * jnp.exp(m_all - m_back)
    for p4 in range(16):
        mine = owner == float(4 * p4)
        tz[0, 1, p4:p4 + 1, :] = jnp.sum(jnp.where(mine, z_all, 0.0), axis=0, keepdims=True)

    for dz in RING:
        pltpu.make_async_remote_copy(
            src_ref=tz.at[0], dst_ref=tz.at[8 - dz], send_sem=s_tzs, recv_sem=s_tzr,
            device_id=zdev(dz), device_id_type=MESH,
        ).start()
    place = lax.broadcasted_iota(jnp.int32, (16, 128), 1) % 32
    filled = jnp.zeros((16, 128), F32)
    for pos in range(8):
        filled = jnp.where(place // 4 == pos, slz[pos, 8:24, :], filled)
    pltpu.make_async_copy(tz.at[1:8], tz.at[1:8], s_tzr).wait()

    def aligned(dz, what):
        t = tz[dz, what]
        if dz == 0:
            return t
        turn = 4 * dz
        return jnp.where(place >= turn, pltpu.roll(t, turn, 1), pltpu.roll(t, 96 + turn, 1))

    tops = [aligned(dz, 0) for dz in range(8)]
    highest = tops[0]
    for t in tops[1:]:
        highest = jnp.maximum(highest, t)
    summed = jnp.zeros((16, 128), F32)
    for dz in range(8):
        summed += aligned(dz, 1) * jnp.exp(tops[dz] - highest)
    log_total = jnp.log(summed)
    norm = jnp.where(filled > 0.5, highest + log_total, EMPTY_NORM)

    turned = jnp.zeros((128, 128), F32)
    for p4 in range(16):
        turned = jnp.where(owner == float(4 * p4), norm[p4:p4 + 1, :], turned)
    back = turned[0:32]
    for k in (1, 2, 3):
        back += pltpu.roll(turned[32 * k:32 * k + 32], 128 - 32 * k, 1)
    for d in range(32):
        lt[d, 0:1, :] = back[d:d + 1, :]
    lr[my_u] = lt[my_u]

    for t in PLANE:
        dev, u = plane(t)
        send(lt.at[u], lr.at[my_u], s_ls, s_lr, dev)

    slot_i = slz[1, 0:1, :].astype(jnp.int32)
    lane_of = ((slot_i // 4) % 4) * 32 + 4 + slot_i % 4
    choose = jnp.where(sub == jnp.broadcast_to(lane_of, (128, 128)), 1.0, 0.0)
    by_lane = jnp.dot(
        log_total, choose, preferred_element_type=F32, precision=lax.Precision.HIGHEST
    )
    p4_row = lax.broadcasted_iota(jnp.int32, (16, 128), 0)
    spread[0:1, :] = jnp.sum(
        jnp.where(p4_row == jnp.broadcast_to(slot_i // 16, (16, 128)), by_lane, 0.0),
        axis=0, keepdims=True,
    )

    pltpu.make_async_copy(lr.at[0:31], lr.at[0:31], s_lr).wait()

    turned = jnp.concatenate(
        [lr[u, 0:1, :] if u == 0 else pltpu.roll(lr[u, 0:1, :], 4 * u, 1) for u in range(32)], axis=0
    )
    for j in range(OWN):
        for tau, pos in enumerate(ORDER):
            got = jnp.where(window == 8 * j + pos, turned, 0.0)
            got = jnp.sum(got, axis=0, keepdims=True)
            turn = 32 * j + 4 * pos
            ss[j, tau:tau + 1, :] = pltpu.roll(got, 128 - turn, 1) if turn else got
    own_col = pl.multiple_of(c * HALF, HALF)
    far_col = pl.multiple_of((1 - c) * HALF, HALF)

    def update(j, carry):
        factor = jnp.exp(ms[j] - ss[j])
        mass = jnp.zeros((BS, 128), F32)
        for n in range(4):
            for h in range(2):
                v = 2 * n + h
                w = e_sc[j, n, :, h * 128:(h + 1) * 128] * factor[v:v + 1, :]
                mass += w
                wb[j, :, v * 128:(v + 1) * 128] = w.astype(BF16)
        denom = jnp.sum(mass, axis=1, keepdims=True) + LAMBDA
        rows = pl.ds(pl.multiple_of(j * BS, BS), BS)
        dn[rows, :] = jnp.broadcast_to(denom, (BS, 128))
        sums = jnp.dot(wb[j], inc[j, :, pl.ds(far_col, HALF)], preferred_element_type=F32)
        prev = ce[rows, pl.ds(far_col, HALF)].astype(F32)
        fr[rows, :] = (sums + LAMBDA * prev) / denom
        at = pl.ds(pl.multiple_of((c * OWN + j) * BS, BS), BS)
        send(fr.at[rows], out.at[at], s_fs, s_fr, (dp, 1 - c))
        return carry

    def update_own(j, carry):
        rows = pl.ds(pl.multiple_of(j * BS, BS), BS)
        at = pl.ds(pl.multiple_of((c * OWN + j) * BS, BS), BS)
        sums = jnp.dot(wb[j], inc[j, :, pl.ds(own_col, HALF)], preferred_element_type=F32)
        prev = ce[rows, pl.ds(own_col, HALF)].astype(F32)
        out[at, :] = (sums + LAMBDA * prev) / dn[rows, 0:1]
        return carry

    lax.fori_loop(0, OWN, update, 0)
    lax.fori_loop(0, OWN, update_own, 0)

    arrived(fr, s_fs)
    arrived(fr, s_fr)
    arrived(raw.at[0:7, 0, 0:ZF], s_zs)
    arrived(raw.at[:, 1:4, 0:ZF], s_as)
    arrived(raw.at[1, 1:4, ZF:ROWS], s_bs)
    arrived(raw.at[0:7, :, ZF:ROWS], s_ys)
    arrived(slz.at[0:7], s_slzs)
    arrived(slp, s_slps)
    arrived(pk.at[:, 1:8], s_ps)
    arrived(stt.at[0:31], s_sts)
    arrived(tz.at[1:8], s_tzs)
    arrived(lt.at[0:31], s_ls)


def local(embeddings, parents, block_lists, centroids):
    dma, vmem = pltpu.SemaphoreType.DMA, pltpu.VMEM
    fresh, spread = pl.pallas_call(
        kernel,
        out_shape=(
            jax.ShapeDtypeStruct((2 * OWN * BS, HALF), F32),
            jax.ShapeDtypeStruct((1, ROWS), F32),
        ),
        in_specs=[pl.BlockSpec(memory_space=pltpu.HBM)] * 4,
        out_specs=(pl.BlockSpec(memory_space=vmem), pl.BlockSpec(memory_space=vmem)),
        scratch_shapes=[
            vmem((8, 4, ROWS, D), BF16),
            vmem((8, 24, 128), F32),
            vmem((3, 8, 8, 128), F32),
            vmem((8, 8, OWN, 16, D), BF16),
            vmem((OWN, 1024, D), BF16),
            vmem((OWN * BS, D), BF16),
            vmem((OWN, 4, BS, 256), F32),
            vmem((OWN, 8, 128), F32),
            vmem((OWN, 8, 128), F32),
            vmem((32, 8, 128), F32),
            vmem((32, 8, 128), F32),
            vmem((8, 2, 16, 128), F32),
            vmem((32, 8, 128), F32),
            vmem((32, 8, 128), F32),
            vmem((OWN, BS, 1024), BF16),
            vmem((OWN * BS, 128), F32),
            vmem((OWN * BS, HALF), F32),
            vmem((512, 128), F32),
            vmem((128, 128), F32),
            vmem((1, ROWS), jnp.int32),
            vmem((16, 64), jnp.int32),
            dma((3,)), dma, dma((8,)), dma, dma((4, 8)), dma, dma, dma, dma((8,)),
            dma, dma, dma, dma,
            dma, dma((8,)), dma((8,)), dma, dma, dma, dma, dma, dma, dma, dma, dma,
        ],
        compiler_params=pltpu.CompilerParams(
            collective_id=0, has_side_effects=True, vmem_limit_bytes=48 * 1024 * 1024
        ),
        cost_estimate=pl.CostEstimate(
            flops=8_000_000_000, bytes_accessed=10_000_000, transcendentals=1_000_000
        ),
        name="kmeans_step",
    )(
        embeddings,
        parents.reshape(1, ROWS),
        block_lists.T,
        centroids,
    )
    return fresh, spread.reshape(ROWS)


def solution(mesh):
    placed = (P(("dp", "rep"), None), P(("dp", "rep")), P(), P("dp", None))
    return jax.shard_map(
        local,
        mesh=mesh,
        in_specs=placed,
        out_specs=(P("dp", "rep"), P(("dp", "rep"))),
        check_vma=False,
    )
```
